128 devices in a mesh: ctx: 8 (over y, z_hi), sess: 16 (over z_lo, x, core).
Axes of the slice: x: 4, y: 4, z: 4 (z_hi: 2, z_lo: 2; z = z_hi * 2 + z_lo), core: 2. Of those that a mesh axis runs over, the one named last changes fastest.
Arguments:
- mel_in: bfloat16 [196608, 128], P(('ctx', 'sess')), may hold values from -6 to 6
- route: int32 [196608], P(('ctx', 'sess')), may hold values from 0 to 1535, as said below
- lengths: int32 [16], replicated, may hold values from 1 to 3072, 24576 in all
- conv_first: bfloat16 [9, 128], replicated, may hold values from -2 to 2
- conv_second: bfloat16 [1152, 128], replicated, may hold values from -0.1875 to 0.1875
- lin_in: bfloat16 [4096, 1536], replicated, may hold values from -0.1875 to 0.1875
- wq: bfloat16 [1536, 768], P('sess'), may hold values from -4.8989795 to 4.8989795
- wk: bfloat16 [1536, 768], P('sess'), may hold values from -0.15309311 to 0.15309311
- wv: bfloat16 [1536, 768], P('sess'), may hold values from -0.15625 to 0.15625
- wo: bfloat16 [768, 1536], P('sess'), may hold values from -0.21875 to 0.21875
- pw1: bfloat16 [1536, 3072], P('sess'), may hold values from -0.15625 to 0.15625
- dw_kernel: bfloat16 [31, 1536], replicated, may hold values from -1 to 1
Outputs:
- encoded: bfloat16 [16, 3072, 1536], P('sess', 'ctx')
The draws below stay inside these ranges and needn't reach their ends.
Inputs may be any that keep to these rules, and one draw needn't show every extreme that they name: `route`: for each device j, the positions carried by the rows bound for j from all devices form a permutation of 0 to 1535.
All inputs are finite; a program needn't handle non-finite values.
Results may differ from the reference program's by a relative error of at most 0.014.
Values may be sent and summed in bfloat16 or wider, within the bound.
A program may use at most 192 MiB of HBM per device.

```python
import math
import jax
import jax.numpy as jnp
import numpy as np
from jax import lax

MEL = 128
CHAN = 128
D = 1536
HEADS = 8
HEAD = 96
KERNEL = 31
MEL_ROWS = 1536
RANKS = 128
SLOT = 12
SESSIONS = 16
LENGTH = 3072


def shared_keys(key):
    base = jax.random.truncated_normal(key, -6.0, 6.0, (D, HEADS * HEAD), jnp.float32)
    return base / math.sqrt(D)


def draw_wk(key, part):
    base = shared_keys(key)
    return base.astype(jnp.bfloat16)


def draw_wq(key, part):
    key = jax.random.fold_in(key, 7)
    own_part = jax.random.truncated_normal(jax.random.fold_in(key, 1), -6.0, 6.0, (D, HEADS * HEAD), jnp.float32) / math.sqrt(D)
    result = 3.0 * own_part
    return result.astype(jnp.bfloat16)


def one_order(order_key):
    return jax.random.permutation(order_key, MEL_ROWS)


def draw_route(key, part):
    key = jax.random.fold_in(key, 3)
    order_keys = jax.random.split(key, RANKS)
    orders = jax.vmap(one_order)(order_keys)
    orders = orders.reshape(RANKS, RANKS, SLOT)
    return jnp.transpose(orders, (1, 0, 2)).reshape(RANKS * MEL_ROWS).astype(jnp.int32)


def level_of(key, extent, cuts, least, top_value):
    gain = 1.0
    for dim, shards_of in cuts:
        draws = jax.random.uniform(jax.random.fold_in(jax.random.fold_in(key, 6), dim), (shards_of,), jnp.float32, least / len(cuts), top_value / len(cuts))
        gain = gain * jnp.repeat(jnp.exp(draws), extent[dim] // shards_of).reshape((-1,) + (1,) * (len(extent) - 1 - dim))
    return gain


def length_profile(number_of, total, most, slope):
    weights = [(1 << 20) // math.isqrt(standing ** slope) + 1 for standing in range(2, number_of + 1)]
    rest, given = total - most - (number_of - 1), [1] * (number_of - 1)
    while rest > 0:
        free = [i for i in range(number_of - 1) if given[i] < most]
        mass, remaining = sum([weights[i] for i in free]), rest
        for i in free:
            more = min(most - given[i], max(1, remaining * weights[i] // mass), rest)
            given[i] = given[i] + more
            rest = rest - more
    return np.array([most] + given)


def uneven_parts(key, amount, total, most, skew):
    if amount == 2:
        one = jax.random.randint(key, (), max(1, total - most), min(most, total - 1) + 1)
        return jnp.stack([one, total - one])
    sizes = jnp.asarray(length_profile(amount, total, most, skew), jnp.int32)
    pairs = (amount - 1) // 2
    donor, sink = sizes[1:1 + 2 * pairs:2], sizes[2:2 + 2 * pairs:2]
    room = jnp.minimum(donor - 1, most - sink)
    passed = jax.random.randint(jax.random.fold_in(key, 1), (pairs,), 0, 1 << 20) % (room + 1)
    sizes = sizes.at[1:1 + 2 * pairs:2].set(donor - passed).at[2:2 + 2 * pairs:2].set(sink + passed)
    return sizes[jax.random.permutation(jax.random.fold_in(key, 2), amount)]


def noise(own_key, extent, spread, limit, shards=(), kind=jnp.bfloat16):
    factor_of = level_of(own_key, extent, shards, -0.22, 0.18) if shards else 1.0
    values = jax.random.normal(own_key, extent, jnp.float32) * spread * factor_of
    return jnp.minimum(jnp.maximum(values, -limit), limit).astype(kind)


def setup_inputs(seed: int = 0) -> dict:
    key_list = jax.random.split(jax.random.key(seed), 13)
    return {
        "mel_in": noise(key_list[0], (RANKS * MEL_ROWS, MEL), 1.0, 6.0, ((0, 128),)),
        "route": draw_route(jax.random.fold_in(key_list[12], 71), 0),
        "lengths": uneven_parts(key_list[2], SESSIONS, SESSIONS * LENGTH // 2, LENGTH, 2).astype(jnp.int32),
        "conv_first": noise(key_list[3], (9, CHAN), 9 ** -0.5, 2.0),
        "conv_second": noise(key_list[4], (9 * CHAN, CHAN), (9 * CHAN) ** -0.5, 0.1875),
        "lin_in": noise(key_list[5], (MEL * CHAN // 4, D), (MEL * CHAN // 16) ** -0.5, 0.1875),
        "wq": draw_wq(jax.random.fold_in(key_list[12], 71), 0),
        "wk": draw_wk(jax.random.fold_in(key_list[12], 71), 0),
        "wv": noise(key_list[8], (D, HEADS * HEAD), D ** -0.5, 0.15625, ((0, 16),)),
        "wo": noise(key_list[9], (HEADS * HEAD, D), (HEADS * HEAD) ** -0.5, 0.21875, ((0, 16),)),
        "pw1": noise(key_list[10], (D, 2 * D), D ** -0.5, 0.15625, ((0, 16),)),
        "dw_kernel": noise(key_list[11], (KERNEL, D), KERNEL ** -0.5, 1.0),
    }


eps = 1e-05

def first_conv(padded, kernel):
    row_count = (padded.shape[0] - 1) // 2
    bin_count = padded.shape[1]
    widened = jnp.pad(padded, ((0, 0), (1, 1)))
    running = jnp.zeros((row_count, bin_count // 2, kernel.shape[1]), jnp.float32)
    for a in range(3):
        for b in range(3):
            tap_rows = widened[a:a + 2 * row_count:2, b:b + bin_count:2].astype(jnp.float32)
            running = running + tap_rows[:, :, None] * kernel[3 * a + b].astype(jnp.float32)[None, None, :]
    return jnp.maximum(running, 0.0).astype(jnp.bfloat16)

def second_conv(padded, kernel):
    row_count = (padded.shape[0] - 1) // 2
    bin_count = padded.shape[1]
    channels = padded.shape[2]
    widened = jnp.pad(padded, ((0, 0), (1, 1), (0, 0)))
    tap_list = [widened[a:a + 2 * row_count:2, b:b + bin_count:2] for a in range(3) for b in range(3)]
    patches = jnp.concatenate(tap_list, axis=2).reshape(row_count * (bin_count // 2), 9 * channels)
    running = jnp.dot(patches, kernel, preferred_element_type=jnp.float32)
    return jnp.maximum(running, 0.0).astype(jnp.bfloat16).reshape(row_count, bin_count // 2 * channels)

def layer_norm(rows_in):
    values = rows_in.astype(jnp.float32)
    row_mean = lax.optimization_barrier(jnp.mean(values, axis=-1, keepdims=True))
    centred = values - row_mean
    variance = lax.optimization_barrier(jnp.mean(centred * centred, axis=-1, keepdims=True))
    return (centred * lax.rsqrt(variance + eps)).astype(jnp.bfloat16)

def depthwise(extended, kernel, row_count):
    running = jnp.zeros((row_count, extended.shape[1]), jnp.float32)
    for j in range(kernel.shape[0]):
        running = running + extended[j:j + row_count].astype(jnp.float32) * kernel[j].astype(jnp.float32)[None, :]
    return running

def attend(queries, key_rows, values, length):
    row_count = queries.shape[0]
    score_scale = 1.0 / math.sqrt(HEAD)
    is_valid = jnp.arange(key_rows.shape[0], dtype=jnp.int32) < length
    head_query = queries.reshape(row_count, HEADS, HEAD).transpose(1, 0, 2)
    head_keys = key_rows.reshape(-1, HEADS, HEAD).transpose(1, 0, 2)
    head_values = values.reshape(-1, HEADS, HEAD).transpose(1, 0, 2)

    def one_head(head_group):
        query_part, key_part, value_part = head_group
        scores = jnp.dot(query_part, key_part.T, preferred_element_type=jnp.float32) * score_scale
        row_max = lax.optimization_barrier(jnp.max(jnp.where(is_valid[None, :], scores, -1e+30), axis=1, keepdims=True))
        weights = jnp.where(is_valid[None, :], jnp.exp(scores - row_max), 0.0).astype(jnp.bfloat16)
        weight_sum = lax.optimization_barrier(jnp.sum(weights.astype(jnp.float32), axis=1, keepdims=True))
        return jnp.dot(weights, value_part, preferred_element_type=jnp.float32) / weight_sum
    head_output = lax.map(one_head, (head_query, head_keys, head_values))
    return head_output.transpose(1, 0, 2).reshape(row_count, HEADS * HEAD).astype(jnp.bfloat16)

def reference(mel_in, route, lengths, conv_first, conv_second, lin_in, wq, wk, wv, wo, pw1, dw_kernel):
    row_index = jnp.arange(RANKS * MEL_ROWS, dtype=jnp.int32)
    target_rank = row_index // SLOT % RANKS
    cycle_pos = target_rank // SESSIONS
    session_id = target_rank % SESSIONS
    target = session_id * (4 * LENGTH) + cycle_pos * MEL_ROWS + route.astype(jnp.int32)
    sessions_mel = jnp.zeros((SESSIONS * 4 * LENGTH, MEL), mel_in.dtype).at[target].set(mel_in)
    sessions_mel = sessions_mel.reshape(SESSIONS, 4 * LENGTH, MEL)

    def one_session(session_pair):
        mel, length = session_pair
        padded = jnp.concatenate([jnp.zeros((3, MEL), mel.dtype), mel], axis=0)
        first_out = first_conv(padded, conv_first)
        second_out = second_conv(first_out, conv_second)
        embedded = jnp.dot(second_out, lin_in, preferred_element_type=jnp.float32).astype(jnp.bfloat16)
        normed = layer_norm(embedded)
        queries = jnp.dot(normed, wq, preferred_element_type=jnp.float32).astype(jnp.bfloat16)
        key_rows = jnp.dot(normed, wk, preferred_element_type=jnp.float32).astype(jnp.bfloat16)
        values = jnp.dot(normed, wv, preferred_element_type=jnp.float32).astype(jnp.bfloat16)
        context = attend(queries, key_rows, values, length)
        residual = (embedded.astype(jnp.float32) + jnp.dot(context, wo, preferred_element_type=jnp.float32)).astype(jnp.bfloat16)
        normed_again = layer_norm(residual)
        lifted = jnp.dot(normed_again, pw1, preferred_element_type=jnp.float32)
        gated_rows = lifted[:, :D] * jax.nn.sigmoid(lifted[:, D:])
        position = jnp.arange(LENGTH, dtype=jnp.int32)
        gated_rows = jnp.where((position < length)[:, None], gated_rows, 0.0).astype(jnp.bfloat16)
        extended = jnp.pad(gated_rows, ((KERNEL // 2, KERNEL // 2), (0, 0)))
        depth_out = depthwise(extended, dw_kernel, LENGTH)
        return (residual.astype(jnp.float32) + depth_out * jax.nn.sigmoid(depth_out)).astype(jnp.bfloat16)
    return lax.map(one_session, (sessions_mel, lengths.astype(jnp.int32)))
```

```python
import functools
import math

import jax
import jax.numpy as jnp
from jax import lax
from jax.experimental import pallas as pl
from jax.experimental.pallas import tpu as pltpu
from jax.sharding import PartitionSpec as P

HEADS = 8
HEAD = 96
KERNEL = 31
EPS = 1e-05
ROWS = 384
PAD = 16
SLOT = 12
RANKS = 128
D = 1536
F32 = jnp.float32
BF16 = jnp.bfloat16
VMEM = pltpu.VMEM
MIB = 1024 * 1024


def vspec():
    return pl.BlockSpec(memory_space=pltpu.VMEM)


def dot(a, b):
    return jnp.dot(a, b, preferred_element_type=F32)


def iota(shape, dim):
    return lax.broadcasted_iota(jnp.int32, shape, dim)


def layer_norm(values):
    row_mean = jnp.mean(values, axis=-1, keepdims=True)
    centred = values - row_mean
    variance = jnp.mean(centred * centred, axis=-1, keepdims=True)
    return (centred * lax.rsqrt(variance + EPS)).astype(BF16)


def place_kernel(arrived, out, wide, sorted_rows):
    wide[...] = arrived[...].astype(F32)
    high = wide[pl.ds(SLOT, RANKS, stride=16), :]
    low = wide[pl.ds(SLOT + 1, RANKS, stride=16), :]
    position = (high * 64.0 + low).T
    for r in range(SLOT):
        sorted_rows[r * RANKS : (r + 1) * RANKS, :] = wide[pl.ds(r, RANKS, stride=16), :].astype(BF16)
    target = iota((ROWS, RANKS), 0).astype(F32) * 4.0
    for k in range(4):
        chosen = jnp.concatenate(
            [
                jnp.where(position[r : r + 1, :] == target + float(k), 1.0, 0.0).astype(BF16)
                for r in range(SLOT)
            ],
            axis=1,
        )
        out[:, 128 * k : 128 * (k + 1)] = dot(chosen, sorted_rows[...]).astype(BF16)


def place(arrived):
    return pl.pallas_call(
        place_kernel,
        out_shape=jax.ShapeDtypeStruct((ROWS, 512), BF16),
        in_specs=[vspec()],
        out_specs=vspec(),
        scratch_shapes=[VMEM((16 * RANKS, 128), F32), VMEM((SLOT * RANKS, 128), BF16)],
        compiler_params=pltpu.CompilerParams(vmem_limit_bytes=24 * MIB),
        name="place_frames",
    )(arrived)


def conv_kernel(
    x, halo, first, second, lin_hbm,
    emb_out, norm_out,
    lin, last, sel, win_e, win_o, band, taps, even, odd, behind, sub, sem,
):
    copy = pltpu.make_async_copy(lin_hbm, lin, sem)
    copy.start()
    total = ROWS + PAD
    row = iota((384, 512), 0)
    col = iota((384, 512), 1)
    a = row // 128
    m = row % 128
    p = col // 32
    r = col % 32
    a2 = jnp.where(r >= 9, 1, 0) + jnp.where(r >= 18, 1, 0)
    i = r - 9 * a2
    hit = (r < 27) & (a == a2) & (m == 8 * p - 1 + i)
    sel[...] = jnp.where(hit, 1.0, 0.0).astype(BF16)
    brow = iota((128, 128), 0)
    kern = first[...].astype(F32)
    for f in range(16):
        block = jnp.zeros((128, 128), F32)
        for tap in range(9):
            at = 32 * (f // 4) + 9 * (tap // 3) + 2 * (f % 4) + tap % 3
            block = jnp.where(brow == at, kern[tap : tap + 1, :], block)
        band[:, 128 * f : 128 * (f + 1)] = block.astype(BF16)
    taps[...] = jnp.zeros_like(taps)
    for place_of, row_tap in enumerate((1, 2, 0)):
        for o in range(2):
            for b in range(3):
                at = 640 * place_of + 128 * (2 * o + b)
                source = (3 * row_tap + b) * 128
                taps[at : at + 128, 128 * o : 128 * (o + 1)] = second[source : source + 128, :]

    last[0:PAD, :] = halo[:, 384:512].astype(F32)
    last[PAD:total, :] = x[:, 384:512].astype(F32)
    previous = last[pl.ds(PAD - 1, ROWS), :].astype(BF16)
    win_e[...] = dot(jnp.concatenate([previous, x[:, 0:256]], axis=1), sel[...]).astype(BF16)
    win_o[0:PAD, :] = dot(halo[:, 128:512], sel[...]).astype(BF16)
    win_o[PAD:total, :] = dot(x[:, 128:512], sel[...]).astype(BF16)
    even[:, 0:128] = jnp.zeros((ROWS, 128), BF16)
    odd[:, 0:128] = jnp.zeros((total, 128), BF16)

    def group(g, carry):
        q = pl.multiple_of((g // 4) * 128, 128)
        bcol = pl.multiple_of((g % 4) * 512, 512)
        to = pl.multiple_of(128 + g * 512, 128)
        weights = band[:, pl.ds(bcol, 512)]
        even[:, pl.ds(to, 512)] = jnp.maximum(dot(win_e[:, pl.ds(q, 128)], weights), 0.0).astype(BF16)
        odd[:, pl.ds(to, 512)] = jnp.maximum(dot(win_o[:, pl.ds(q, 128)], weights), 0.0).astype(BF16)
        at = pl.multiple_of(g * 512, 512)
        odd_part = odd[:, pl.ds(at, 640)]
        behind[...] = dot(odd_part, taps[1280:1920, :])
        both = jnp.concatenate([even[:, pl.ds(at, 640)], odd[PAD:total, pl.ds(at, 640)]], axis=1)
        here = dot(both, taps[0:1280, :]) + behind[pl.ds(PAD - 1, ROWS), :]
        sub[:, pl.ds(pl.multiple_of(g * 256, 256), 256)] = jnp.maximum(here, 0.0).astype(BF16)
        return carry

    lax.fori_loop(0, 16, group, 0)
    copy.wait()

    def project(n, carry):
        at = pl.multiple_of(n * 512, 512)
        emb_out[:, pl.ds(at, 512)] = dot(sub[...], lin[:, pl.ds(at, 512)]).astype(BF16)
        return carry

    lax.fori_loop(0, 3, project, 0)
    norm_out[...] = layer_norm(emb_out[...].astype(F32))


def convolve(x, halo, first, second, lin_in):
    total = ROWS + PAD
    return pl.pallas_call(
        conv_kernel,
        out_shape=[jax.ShapeDtypeStruct((ROWS, D), BF16)] * 2,
        in_specs=[vspec()] * 4 + [pl.BlockSpec(memory_space=pl.ANY)],
        out_specs=[vspec()] * 2,
        scratch_shapes=[
            VMEM((4096, D), BF16),
            VMEM((total, 128), F32),
            VMEM((384, 512), BF16),
            VMEM((ROWS, 512), BF16),
            VMEM((total, 512), BF16),
            VMEM((128, 2048), BF16),
            VMEM((1920, 256), BF16),
            VMEM((ROWS, 8320), BF16),
            VMEM((total, 8320), BF16),
            VMEM((total, 256), F32),
            VMEM((ROWS, 4096), BF16),
            pltpu.SemaphoreType.DMA,
        ],
        compiler_params=pltpu.CompilerParams(vmem_limit_bytes=52 * MIB),
        cost_estimate=pl.CostEstimate(flops=14_000_000_000, bytes_accessed=14_000_000, transcendentals=0),
        name="subsample",
    )(x, halo, first, second, lin_in)


def qkv_kernel(live_rows, normed, weights, out):
    lane = iota((ROWS, 128), 1)
    live = iota((ROWS, 128), 0) < live_rows[0]
    for part in range(3):
        rows = dot(normed[...], weights[:, 768 * part : 768 * (part + 1)])
        if part == 1:
            extra = jnp.where(live, 0.0, -1e30)
        else:
            extra = jnp.ones((ROWS, 128), F32)
        for h in range(HEADS):
            base, shift = (96 * h) // 128 * 128, (96 * h) % 128
            if shift == 0:
                head = rows[:, base : base + 128]
            elif shift == 32:
                head = pltpu.roll(rows[:, base : base + 128], 128 - shift, 1)
            else:
                head = pltpu.roll(rows[:, base : base + 256], 256 - shift, 1)[:, 0:128]
            head = jnp.where(lane < HEAD, head, jnp.where(lane == HEAD, extra, 0.0))
            out[h, :, 128 * part : 128 * (part + 1)] = head.astype(BF16)


def qkv(live_rows, normed, weights):
    return pl.pallas_call(
        qkv_kernel,
        out_shape=jax.ShapeDtypeStruct((HEADS, ROWS, 384), BF16),
        in_specs=[pl.BlockSpec(memory_space=pltpu.SMEM), vspec(), vspec()],
        out_specs=vspec(),
        compiler_params=pltpu.CompilerParams(vmem_limit_bytes=40 * MIB),
        cost_estimate=pl.CostEstimate(flops=2_700_000_000, bytes_accessed=10_000_000, transcendentals=0),
        name="project_heads",
    )(live_rows, normed, weights)


QBLOCK = 256


def attend_kernel(queries, rows, out):
    keys = rows[:, 128:256]
    scores = lax.dot_general(
        queries[:, 0:128], keys, (((1,), (1,)), ((), ())), preferred_element_type=F32
    )
    scale = math.log2(math.e) / math.sqrt(HEAD)
    row_max = jnp.max(scores, axis=1, keepdims=True)
    weights = jnp.exp2((scores - row_max) * scale).astype(BF16)
    total = dot(weights, rows[:, 256:384])
    lane = iota(total.shape, 1)
    result = total / total[:, HEAD : HEAD + 1]
    out[...] = jnp.where(lane < HEAD, result, 0.0).astype(BF16)


def attend(rows):
    count = rows.shape[0]
    return pl.pallas_call(
        attend_kernel,
        grid=(count // QBLOCK,),
        out_shape=jax.ShapeDtypeStruct((count, 128), BF16),
        in_specs=[
            pl.BlockSpec((QBLOCK, 384), lambda i: (i, 0)),
            vspec(),
        ],
        out_specs=pl.BlockSpec((QBLOCK, 128), lambda i: (i, 0)),
        compiler_params=pltpu.CompilerParams(vmem_limit_bytes=40 * MIB),
        cost_estimate=pl.CostEstimate(flops=5_000_000_000, bytes_accessed=4_000_000, transcendentals=9_400_000),
        name="attend_head",
    )(rows, rows)


def gate_kernel(live_rows, heads, emb, gathered, residual_out, gated_out, w_out):
    for s in range(16):
        for half in range(2):
            block = gathered[96 * s + 48 * half : 96 * s + 48 * (half + 1), 3072:3840]
            w_out[48 * s : 48 * (s + 1), 768 * half : 768 * (half + 1)] = block
    w_out[768:800, :] = jnp.zeros((32, D), BF16)
    total = emb[...].astype(F32)
    for pair in range(4):
        left = jnp.concatenate([heads[2 * pair], heads[2 * pair + 1]], axis=1)
        at = 192 * pair
        right = jnp.concatenate([w_out[at : at + 128, :], w_out[at + 96 : at + 224, :]], axis=0)
        total = total + dot(left, right)
    residual = total.astype(BF16)
    residual_out[...] = residual
    normed = layer_norm(residual.astype(F32))
    live = iota((ROWS, 256), 0) < live_rows[0]
    for n in range(6):
        value = dot(normed, gathered[:, 256 * n : 256 * (n + 1)])
        gate = dot(normed, gathered[:, D + 256 * n : D + 256 * (n + 1)])
        gated = jnp.where(live, value * jax.nn.sigmoid(gate), 0.0)
        gated_out[:, 256 * n : 256 * (n + 1)] = gated.astype(BF16)


def gate(live_rows, heads, emb, gathered):
    return pl.pallas_call(
        gate_kernel,
        out_shape=[jax.ShapeDtypeStruct((ROWS, D), BF16)] * 2,
        in_specs=[pl.BlockSpec(memory_space=pltpu.SMEM), vspec(), vspec(), vspec()],
        out_specs=[vspec()] * 2,
        scratch_shapes=[VMEM((800, D), BF16)],
        compiler_params=pltpu.CompilerParams(vmem_limit_bytes=48 * MIB),
        cost_estimate=pl.CostEstimate(flops=4_600_000_000, bytes_accessed=15_000_000, transcendentals=600_000),
        name="gate_rows",
    )(live_rows, heads, emb, gathered)


def depth_kernel(low, gated, high, residual, kernel, out, wide):
    wide[0:PAD, :] = low[...].astype(F32)
    wide[PAD : PAD + ROWS, :] = gated[...].astype(F32)
    wide[PAD + ROWS :, :] = high[...].astype(F32)
    weights = kernel[...].astype(F32)
    chunk = 64
    for start in range(0, ROWS, chunk):
        total = jnp.zeros((chunk, 128), F32)
        for j in range(KERNEL):
            total = total + wide[pl.ds(start + j + 1, chunk), :] * weights[j : j + 1, :]
        rows = residual[start : start + chunk, :].astype(F32) + total * jax.nn.sigmoid(total)
        out[start : start + chunk, :] = rows.astype(BF16)


def depthwise(low, gated, high, residual, kernel):
    column = lambda rows: pl.BlockSpec((rows, 128), lambda n: (0, n))
    return pl.pallas_call(
        depth_kernel,
        grid=(D // 128,),
        out_shape=jax.ShapeDtypeStruct((ROWS, D), BF16),
        in_specs=[column(PAD), column(ROWS), column(PAD), column(ROWS), column(32)],
        out_specs=column(ROWS),
        scratch_shapes=[VMEM((ROWS + 2 * PAD, 128), F32)],
        compiler_params=pltpu.CompilerParams(vmem_limit_bytes=24 * MIB),
        name="depthwise",
    )(low, gated, high, residual, kernel)


def shifted(block, axis, step):
    count = lax.axis_size(axis)
    route = [(i, i + step) for i in range(count) if 0 <= i + step < count]
    return lax.ppermute(block, axis, route)


def local(mel_in, route, lengths, conv_first, conv_second, lin_in, wq, wk, wv, wo, pw1, dw_kernel):
    w_qkv = lax.all_gather(jnp.concatenate([wq, wk, wv], axis=1), "sess", axis=0, tiled=True)
    tail = jnp.concatenate([pw1, jnp.concatenate([wo[:, :768], wo[:, 768:]], axis=0)], axis=1)
    w_tail = lax.all_gather(tail, "sess", axis=0, tiled=True)

    position = jnp.pad(route.reshape(RANKS, 1, SLOT), ((0, 0), (0, 0), (0, 128 - SLOT)))
    slots = jnp.concatenate(
        [
            mel_in.reshape(RANKS, SLOT, 128),
            (position // 64).astype(BF16),
            (position % 64).astype(BF16),
            jnp.zeros((RANKS, 2, 128), BF16),
        ],
        axis=1,
    )
    arrived = lax.all_to_all(slots, ("ctx", "sess"), split_axis=0, concat_axis=0, tiled=True)
    frames = place(arrived.reshape(16 * RANKS, 128))
    halo = shifted(frames[ROWS - PAD :], "ctx", 1)
    first = jnp.pad(conv_first, ((0, 7), (0, 0)))
    embedded, normed = convolve(frames, halo, first, conv_second, lin_in)

    length = lengths[lax.axis_index("sess")]
    live_rows = (length - lax.axis_index("ctx") * ROWS).reshape(1)
    sent = qkv(live_rows, normed, w_qkv)
    held = lax.all_to_all(sent, "ctx", split_axis=0, concat_axis=0, tiled=True)
    context = attend(held.reshape(HEADS * ROWS, 384))
    heads = lax.all_to_all(context.reshape(HEADS, ROWS, 128), "ctx", split_axis=0, concat_axis=0, tiled=True)
    residual, gated = gate(live_rows, heads, embedded, w_tail)
    low = shifted(gated[ROWS - PAD :], "ctx", 1)
    high = shifted(gated[:PAD], "ctx", -1)
    encoded = depthwise(low, gated, high, residual, jnp.pad(dw_kernel, ((0, 1), (0, 0))))
    return encoded[None]


def solution(mesh):
    return jax.shard_map(
        local,
        mesh=mesh,
        in_specs=(
            P(("ctx", "sess"), None),
            P(("ctx", "sess")),
            P(),
            P(),
            P(),
            P(),
            P("sess", None),
            P("sess", None),
            P("sess", None),
            P("sess", None),
            P("sess", None),
            P(),
        ),
        out_specs=P("sess", "ctx", None),
        check_vma=False,
    )
```

```python
import functools
import math

import jax
import jax.numpy as jnp
from jax import lax
from jax.experimental import pallas as pl
from jax.experimental.pallas import tpu as pltpu
from jax.sharding import PartitionSpec as P

HEADS = 8
HEAD = 96
KERNEL = 31
EPS = 1e-05
ROWS = 384
PAD = 16
SLOT = 12
RANKS = 128
D = 1536
F32 = jnp.float32
BF16 = jnp.bfloat16
VMEM = pltpu.VMEM
DMA = pltpu.SemaphoreType.DMA
MESH = pl.DeviceIdType.MESH
PARTS = 8
MIB = 1024 * 1024


def vspec():
    return pl.BlockSpec(memory_space=pltpu.VMEM)


def dot(a, b):
    return jnp.dot(a, b, preferred_element_type=F32)


def iota(shape, dim):
    return lax.broadcasted_iota(jnp.int32, shape, dim)


def layer_norm(values):
    row_mean = jnp.mean(values, axis=-1, keepdims=True)
    centred = values - row_mean
    variance = jnp.mean(centred * centred, axis=-1, keepdims=True)
    return (centred * lax.rsqrt(variance + EPS)).astype(BF16)


def remote(source, target, send, recv, device):
    return pltpu.make_async_remote_copy(
        src_ref=source, dst_ref=target, send_sem=send, recv_sem=recv, device_id=device, device_id_type=MESH
    )


class Gather:
    def __init__(self, own, full, split, send, recv, here):
        ctx, sess = here
        y, z_hi = ctx // 2, ctx % 2
        z_lo, x, core = sess // 8, (sess // 2) % 4, sess % 2
        z = 2 * z_hi + z_lo

        def device(x_at, z_at, core_at):
            return (2 * y + z_at // 2, (z_at % 2) * 8 + x_at * 2 + core_at)

        self.next, self.prev = device((x + 1) % 4, z, core), device((x + 3) % 4, z, core)
        self.above, self.below = device(x, (z + 1) % 4, core), device(x, (z + 3) % 4, core)
        self.twin = device(x, z, 1 - core)
        self.order = [x, (x + 3) % 4, (x + 1) % 4, (x + 2) % 4]
        self.index = lambda z_at, x_at, core_at: z_at * 8 + x_at * 2 + core_at
        self.z_lo, self.core, self.sess = z_lo, core, sess
        self.own, self.full = own, full
        rows = own.shape[0]
        self.low, self.high = pl.ds(0, split), pl.ds(split, rows - split)
        self.send_sem, self.recv_sem = send, recv
        self.sent = []

    def send(self, source, target, recv, device):
        copy = remote(source, target, self.send_sem.at[len(self.sent)], self.recv_sem.at[recv], device)
        copy.start()
        self.sent.append(copy)

    def pass_on(self, part, recv, device):
        self.send(part, part, recv, device)

    def wait(self, part, recv):
        remote(part, part, self.send_sem.at[0], self.recv_sem.at[recv], self.twin).wait_recv()

    def start(self):
        full, sess = self.full, self.sess
        self.send(self.own, full.at[sess], 0, self.next)
        self.send(self.own, full.at[sess], 1, self.prev)
        self.send(self.own.at[self.low], full.at[sess, self.low], 4, self.above)
        self.send(self.own.at[self.high], full.at[sess, self.high], 5, self.below)
        self.send(self.own, full.at[sess], 12, self.twin)

    def along_x(self):
        full, low, high = self.full, self.low, self.high
        a = self.index(self.z_lo, self.order[1], self.core)
        b = self.index(self.z_lo, self.order[2], self.core)
        self.wait(full.at[a], 0)
        self.pass_on(full.at[a, low], 2, self.next)
        self.wait(full.at[b], 1)
        self.pass_on(full.at[b, high], 3, self.prev)
        for at, recv in ((a, 6), (b, 8)):
            self.pass_on(full.at[at, low], recv, self.above)
            self.pass_on(full.at[at, high], recv + 1, self.below)
        self.pass_on(full.at[a], 13, self.twin)
        self.pass_on(full.at[b], 14, self.twin)

    def across(self):
        full, low, high = self.full, self.low, self.high
        c = self.index(self.z_lo, self.order[3], self.core)
        self.wait(full.at[c, low], 2)
        self.pass_on(full.at[c, low], 10, self.above)
        self.pass_on(full.at[c, low], 15, self.twin)
        self.wait(full.at[c, high], 3)
        self.pass_on(full.at[c, high], 11, self.below)
        self.pass_on(full.at[c, high], 16, self.twin)

    def along_z(self, which):
        full, low, high = self.full, self.low, self.high
        for j in which:
            at = self.index(1 - self.z_lo, self.order[j], self.core)
            self.wait(full.at[at, low], 4 + 2 * j)
            self.pass_on(full.at[at, low], 17 + 2 * j, self.twin)
            self.wait(full.at[at, high], 5 + 2 * j)
            self.pass_on(full.at[at, high], 18 + 2 * j, self.twin)

    def finish(self):
        full, low, high, core = self.full, self.low, self.high, 1 - self.core
        for j in range(3):
            self.wait(full.at[self.index(self.z_lo, self.order[j], core)], 12 + j)
        at = self.index(self.z_lo, self.order[3], core)
        self.wait(full.at[at, low], 15)
        self.wait(full.at[at, high], 16)
        for j in range(4):
            at = self.index(1 - self.z_lo, self.order[j], core)
            self.wait(full.at[at, low], 17 + 2 * j)
            self.wait(full.at[at, high], 18 + 2 * j)

    def drain(self):
        for copy in self.sent:
            copy.wait_send()


GATHER_SENDS = 25
GATHER_RECVS = 25


def merged(block):
    return block.reshape(block.shape[0] * block.shape[1], block.shape[2])


def block_kernel(
    live_rows, slots, first, second, kernel, lin_hbm, qkv_own, tail_own,
    out, tail_full,
    arrived, wide, sorted_rows, frames, halo, last, sel, win_e, win_o, band, taps,
    even, odd, behind, sub, big, emb, normed, w_qkv, sent, held, context, heads,
    residual, gated, edges, deep,
    mel_send, mel_recv, local_sem, halo_send, halo_recv,
    qkv_send, qkv_recv, head_send, head_recv, edge_send, edge_recv,
    gq_send, gq_recv, gt_send, gt_recv,
):
    ctx, sess = lax.axis_index("ctx"), lax.axis_index("sess")
    me = ctx * 16 + sess
    total = ROWS + PAD
    here = (ctx, sess)
    after, before = ((ctx + 1) % PARTS, sess), ((ctx + PARTS - 1) % PARTS, sess)

    barrier = pltpu.get_barrier_semaphore()

    def greet(i, carry):
        other = lax.rem(me + i, RANKS)
        pl.semaphore_signal(barrier, inc=1, device_id=(other // 16, other % 16), device_id_type=MESH)
        return carry

    lax.fori_loop(1, RANKS, greet, 0)
    lin_copy = pltpu.make_async_copy(lin_hbm, big, local_sem.at[0])
    lin_copy.start()
    own_qkv = pltpu.make_async_copy(qkv_own, w_qkv.at[sess], local_sem.at[1])
    own_qkv.start()
    own_tail = pltpu.make_async_copy(tail_own, tail_full.at[sess], local_sem.at[2])
    own_tail.start()
    own_slot = pltpu.make_async_copy(slots.at[me], arrived.at[me], local_sem.at[3])
    own_slot.start()
    prepare(first, second, sel, band, taps)
    pl.semaphore_wait(barrier, RANKS - 1)

    def deliver(i, carry):
        other = lax.rem(me + i, RANKS)
        remote(slots.at[other], arrived.at[me], mel_send, mel_recv, (other // 16, other % 16)).start()
        return carry

    lax.fori_loop(1, RANKS, deliver, 0)
    gather_qkv = Gather(qkv_own, w_qkv, 48, gq_send, gq_recv, here)
    gather_tail = Gather(tail_own, tail_full, 128, gt_send, gt_recv, here)
    gather_qkv.start()
    own_slot.wait()
    all_slots = remote(slots.at[0 : RANKS - 1], arrived.at[0 : RANKS - 1], mel_send, mel_recv, after)
    all_slots.wait_recv()

    place(arrived, wide, sorted_rows, frames)
    halo_copy = remote(frames.at[ROWS - PAD :], halo, halo_send, halo_recv, after)
    halo_copy.start()
    gather_qkv.along_x()
    win_o[PAD:total, :] = dot(frames[:, 128:512], sel[...]).astype(BF16)
    halo_copy.wait_recv()
    first_rows = jnp.where(ctx > 0, halo[...].astype(F32), 0.0)
    last[0:PAD, :] = first_rows[:, 384:512]
    last[PAD:total, :] = frames[:, 384:512].astype(F32)
    previous = last[pl.ds(PAD - 1, ROWS), :].astype(BF16)
    win_e[...] = dot(jnp.concatenate([previous, frames[:, 0:256]], axis=1), sel[...]).astype(BF16)
    win_o[0:PAD, :] = dot(first_rows.astype(BF16)[:, 128:512], sel[...]).astype(BF16)

    def four_bins(g, side):
        q = pl.multiple_of((g // 4) * 128, 128)
        weights = band[:, pl.ds(pl.multiple_of((g % 4) * 512, 512), 512)]
        even[side, :, 128:640] = jnp.maximum(dot(win_e[:, pl.ds(q, 128)], weights), 0.0).astype(BF16)
        odd[side, :, 128:640] = jnp.maximum(dot(win_o[:, pl.ds(q, 128)], weights), 0.0).astype(BF16)
        even[1 - side, :, 0:128] = even[side, :, 512:640]
        odd[1 - side, :, 0:128] = odd[side, :, 512:640]

    def two_bins(g, side):
        behind[...] = dot(odd[side], taps[1280:1920, :])
        both = jnp.concatenate([even[side], odd[side, PAD:total, :]], axis=1)
        rows = dot(both, taps[0:1280, :]) + behind[pl.ds(PAD - 1, ROWS), :]
        sub[:, pl.ds(pl.multiple_of(g * 256, 256), 256)] = jnp.maximum(rows, 0.0).astype(BF16)

    def groups(i, carry):
        four_bins(2 * i, 0)
        two_bins(2 * i, 0)
        four_bins(2 * i + 1, 1)
        two_bins(2 * i + 1, 1)
        return carry

    even[0, :, 0:128] = jnp.zeros((ROWS, 128), BF16)
    odd[0, :, 0:128] = jnp.zeros((total, 128), BF16)
    lax.fori_loop(0, 3, groups, 0)
    gather_qkv.across()
    gather_tail.start()
    lax.fori_loop(3, 6, groups, 0)
    gather_qkv.along_z((0, 1))
    lax.fori_loop(6, 8, groups, 0)
    gather_qkv.along_z((2, 3))
    lin_copy.wait()

    def project(n, carry):
        at = pl.multiple_of(n * 512, 512)
        emb[:, pl.ds(at, 512)] = dot(sub[...], merged(big[:, :, pl.ds(at, 512)])).astype(BF16)
        return carry

    lax.fori_loop(0, 3, project, 0)
    normed[...] = layer_norm(emb[...].astype(F32))
    gather_tail.along_x()

    gather_qkv.finish()
    own_qkv.wait()
    lane = iota((ROWS, 128), 1)
    live = iota((ROWS, 128), 0) < live_rows[0]
    shares = []
    for part in (1, 2, 0):
        rows = dot(normed[...], merged(w_qkv[:, :, 768 * part : 768 * (part + 1)]))
        if part == 1:
            extra = jnp.where(live, 0.0, -1e30)
        else:
            extra = jnp.ones((ROWS, 128), F32)
        for h in range(HEADS):
            base, shift = (96 * h) // 128 * 128, (96 * h) % 128
            if shift == 0:
                head = rows[:, base : base + 128]
            elif shift == 32:
                head = pltpu.roll(rows[:, base : base + 128], 128 - shift, 1)
            else:
                head = pltpu.roll(rows[:, base : base + 256], 256 - shift, 1)[:, 0:128]
            head = jnp.where(lane < HEAD, head, jnp.where(lane == HEAD, extra, 0.0))
            sent[part, h] = head.astype(BF16)
        own = pltpu.make_async_copy(sent.at[part, ctx], held.at[part, ctx], local_sem.at[4 + part])
        own.start()
        shares.append(own)
        for i in range(1, PARTS):
            other = lax.rem(ctx + i, PARTS)
            copy = remote(
                sent.at[part, other], held.at[part, ctx],
                qkv_send.at[part, i], qkv_recv.at[part, i], (other, sess),
            )
            copy.start()
            shares.append(copy)
    gather_tail.across()
    tail_copy = pltpu.make_async_copy(tail_full, big.at[:, 0:240, :], local_sem.at[7])
    for copy in shares:
        copy.wait()
    gather_tail.along_z((0, 1))

    scale = math.log2(math.e) / math.sqrt(HEAD)

    def attend(i, carry):
        other = lax.rem(ctx + i, PARTS)
        keys, values = merged(held[1]), merged(held[2])
        for half in range(2):
            at = pl.ds(half * (ROWS // 2), ROWS // 2)
            scores = lax.dot_general(
                held[0, other, at, :], keys, (((1,), (1,)), ((), ())), preferred_element_type=F32
            )
            row_max = jnp.max(scores, axis=1, keepdims=True)
            weights = jnp.exp2((scores - row_max) * scale).astype(BF16)
            summed = dot(weights, values)
            result = summed / summed[:, HEAD : HEAD + 1]
            result = jnp.where(iota(result.shape, 1) < HEAD, result, 0.0)
            context[other, at, :] = result.astype(BF16)
        return carry

    def attend_for(i, carry):
        attend(i, carry)
        other = lax.rem(ctx + i, PARTS)
        remote(
            context.at[other], heads.at[ctx], head_send.at[i], head_recv.at[i], (other, sess)
        ).start()
        return carry

    lax.fori_loop(1, 5, attend_for, 0)
    gather_tail.along_z((2, 3))
    lax.fori_loop(5, PARTS, attend_for, 0)
    gather_tail.finish()
    own_tail.wait()
    tail_copy.start()
    attend(0, 0)
    own = pltpu.make_async_copy(context.at[ctx], heads.at[ctx], local_sem.at[8])
    own.start()
    own.wait()
    for i in range(1, PARTS):
        other = lax.rem(ctx + i, PARTS)
        remote(context.at[other], heads.at[ctx], head_send.at[i], head_recv.at[i], (other, sess)).wait()
    tail_copy.wait()

    w_out = merged(big[:, 192:240, :])
    summed = emb[...].astype(F32)
    for pair in range(4):
        left = jnp.concatenate([heads[2 * pair], heads[2 * pair + 1]], axis=1)
        at = 192 * pair
        pad = jnp.zeros((32, D), BF16)
        right = jnp.concatenate([w_out[at : at + 96], pad, w_out[at + 96 : at + 192], pad], axis=0)
        summed = summed + dot(left, right)
    residual[...] = summed.astype(BF16)
    normed[...] = layer_norm(residual[...].astype(F32))
    live = iota((ROWS, 256), 0) < live_rows[0]

    def lift(n, carry):
        at = pl.ds(pl.multiple_of(n * 256, 256), 256)
        value = dot(normed[...], merged(big[:, 0:96, at]))
        gate = dot(normed[...], merged(big[:, 96:192, at]))
        rows = jnp.where(live, value * jax.nn.sigmoid(gate), 0.0).astype(BF16)
        gated[:, at] = rows
        deep[PAD : PAD + ROWS, at] = rows.astype(F32)
        return carry

    lax.fori_loop(0, 6, lift, 0)
    to_after = remote(gated.at[ROWS - PAD :], edges.at[0], edge_send.at[0], edge_recv.at[0], after)
    to_before = remote(gated.at[0:PAD], edges.at[1], edge_send.at[1], edge_recv.at[1], before)
    to_after.start()
    to_before.start()

    def taps_of(n, starts):
        at = pl.ds(pl.multiple_of(n * 128, 128), 128)
        weights = kernel[:, at].astype(F32)
        for start in starts:
            rows = jnp.zeros((64, 128), F32)
            for j in range(KERNEL):
                rows = rows + deep[pl.ds(start + j + 1, 64), at] * weights[j : j + 1, :]
            rows = residual[start : start + 64, at].astype(F32) + rows * jax.nn.sigmoid(rows)
            out[start : start + 64, at] = rows.astype(BF16)

    def inner(n, carry):
        taps_of(n, (64, 128, 192, 256))
        return carry

    def outer(n, carry):
        taps_of(n, (0, 320))
        return carry

    lax.fori_loop(0, D // 128, inner, 0)
    to_after.wait_recv()
    to_before.wait_recv()
    deep[0:PAD, :] = jnp.where(ctx > 0, edges[0].astype(F32), 0.0)
    deep[PAD + ROWS :, :] = jnp.where(ctx < PARTS - 1, edges[1].astype(F32), 0.0)
    lax.fori_loop(0, D // 128, outer, 0)

    all_slots.wait_send()
    halo_copy.wait_send()
    to_after.wait_send()
    to_before.wait_send()
    gather_qkv.drain()
    gather_tail.drain()


def prepare(first, second, sel, band, taps):
    row = iota((384, 512), 0)
    col = iota((384, 512), 1)
    a, m, p, r = row // 128, row % 128, col // 32, col % 32
    b = jnp.where(r >= 9, 1, 0) + jnp.where(r >= 18, 1, 0)
    hit = (r < 27) & (a == b) & (m == 8 * p - 1 + r - 9 * b)
    sel[...] = jnp.where(hit, 1.0, 0.0).astype(BF16)
    band_row = iota((128, 128), 0)
    values = first[...].astype(F32)
    for f in range(16):
        block = jnp.zeros((128, 128), F32)
        for tap in range(9):
            at = 32 * (f // 4) + 9 * (tap // 3) + 2 * (f % 4) + tap % 3
            block = jnp.where(band_row == at, values[tap : tap + 1, :], block)
        band[:, 128 * f : 128 * (f + 1)] = block.astype(BF16)
    taps[...] = jnp.zeros_like(taps)
    for position, row_tap in enumerate((1, 2, 0)):
        for o in range(2):
            for c in range(3):
                at = 640 * position + 128 * (2 * o + c)
                source = (3 * row_tap + c) * 128
                taps[at : at + 128, 128 * o : 128 * (o + 1)] = second[source : source + 128, :]


def place(arrived, wide, sorted_rows, frames):
    wide[...] = merged(arrived[...]).astype(F32)
    high = wide[pl.ds(SLOT, RANKS, stride=16), :]
    low = wide[pl.ds(SLOT + 1, RANKS, stride=16), :]
    position = (high * 64.0 + low).T
    for r in range(SLOT):
        sorted_rows[r * RANKS : (r + 1) * RANKS, :] = wide[pl.ds(r, RANKS, stride=16), :].astype(BF16)
    target = iota((ROWS, RANKS), 0).astype(F32) * 4.0
    for k in range(4):
        chosen = jnp.concatenate(
            [
                jnp.where(position[r : r + 1, :] == target + float(k), 1.0, 0.0).astype(BF16)
                for r in range(SLOT)
            ],
            axis=1,
        )
        frames[:, 128 * k : 128 * (k + 1)] = dot(chosen, sorted_rows[...]).astype(BF16)


def block(live_rows, slots, first, second, kernel, lin_in, qkv_own, tail_own):
    total = ROWS + PAD
    anywhere = pl.BlockSpec(memory_space=pl.ANY)
    return pl.pallas_call(
        block_kernel,
        out_shape=[
            jax.ShapeDtypeStruct((ROWS, D), BF16),
            jax.ShapeDtypeStruct((16, 240, D), BF16),
        ],
        in_specs=[pl.BlockSpec(memory_space=pltpu.SMEM)] + [vspec()] * 4 + [anywhere] * 3,
        out_specs=[vspec(), anywhere],
        scratch_shapes=[
            VMEM((RANKS, 16, 128), BF16),
            VMEM((16 * RANKS, 128), F32),
            VMEM((SLOT * RANKS, 128), BF16),
            VMEM((ROWS, 512), BF16),
            VMEM((PAD, 512), BF16),
            VMEM((total, 128), F32),
            VMEM((384, 512), BF16),
            VMEM((ROWS, 512), BF16),
            VMEM((total, 512), BF16),
            VMEM((128, 2048), BF16),
            VMEM((1920, 256), BF16),
            VMEM((2, ROWS, 640), BF16),
            VMEM((2, total, 640), BF16),
            VMEM((total, 256), F32),
            VMEM((ROWS, 4096), BF16),
            VMEM((16, 256, D), BF16),
            VMEM((ROWS, D), BF16),
            VMEM((ROWS, D), BF16),
            VMEM((16, 96, 2304), BF16),
            VMEM((3, HEADS, ROWS, 128), BF16),
            VMEM((3, HEADS, ROWS, 128), BF16),
            VMEM((HEADS, ROWS, 128), BF16),
            VMEM((HEADS, ROWS, 128), BF16),
            VMEM((ROWS, D), BF16),
            VMEM((ROWS, D), BF16),
            VMEM((2, PAD, D), BF16),
            VMEM((ROWS + 2 * PAD, D), F32),
            DMA, DMA, DMA((9,)), DMA, DMA,
            DMA((3, PARTS)), DMA((3, PARTS)), DMA((PARTS,)), DMA((PARTS,)), DMA((2,)), DMA((2,)),
            DMA((GATHER_SENDS,)), DMA((GATHER_RECVS,)), DMA((GATHER_SENDS,)), DMA((GATHER_RECVS,)),
        ],
        compiler_params=pltpu.CompilerParams(
            vmem_limit_bytes=62 * MIB, collective_id=0, has_side_effects=True
        ),
        cost_estimate=pl.CostEstimate(
            flops=27_000_000_000, bytes_accessed=60_000_000, transcendentals=12_000_000
        ),
        name="conformer_block",
    )(live_rows, slots, first, second, kernel, lin_in, qkv_own, tail_own)


def local(mel_in, route, lengths, conv_first, conv_second, lin_in, wq, wk, wv, wo, pw1, dw_kernel):
    qkv_own = jnp.concatenate([wq, wk, wv], axis=1)
    tail_own = jnp.concatenate([pw1[:, :D], pw1[:, D:], wo], axis=0)
    position = jnp.pad(route.reshape(RANKS, 1, SLOT), ((0, 0), (0, 0), (0, 128 - SLOT)))
    slots = jnp.concatenate(
        [
            mel_in.reshape(RANKS, SLOT, 128),
            (position // 64).astype(BF16),
            (position % 64).astype(BF16),
            jnp.zeros((RANKS, 2, 128), BF16),
        ],
        axis=1,
    )
    first = jnp.pad(conv_first, ((0, 7), (0, 0)))
    kernel = jnp.pad(dw_kernel, ((0, 1), (0, 0)))
    length = lengths[lax.axis_index("sess")]
    live_rows = (length - lax.axis_index("ctx") * ROWS).reshape(1)
    encoded, _ = block(
        live_rows, slots, first, conv_second, kernel, lin_in.reshape(16, 256, D), qkv_own, tail_own
    )
    return encoded[None]


def solution(mesh):
    return jax.shard_map(
        local,
        mesh=mesh,
        in_specs=(
            P(("ctx", "sess"), None),
            P(("ctx", "sess")),
            P(),
            P(),
            P(),
            P(),
            P("sess", None),
            P("sess", None),
            P("sess", None),
            P("sess", None),
            P("sess", None),
            P(),
        ),
        out_specs=P("sess", "ctx", None),
        check_vma=False,
    )
```

```python
import functools
import math

import jax
import jax.numpy as jnp
from jax import lax
from jax.experimental import pallas as pl
from jax.experimental.pallas import tpu as pltpu
from jax.sharding import PartitionSpec as P

HEADS = 8
HEAD = 96
KERNEL = 31
EPS = 1e-05
ROWS = 384
PAD = 16
SLOT = 12
RANKS = 128
D = 1536
F32 = jnp.float32
BF16 = jnp.bfloat16
VMEM = pltpu.VMEM
DMA = pltpu.SemaphoreType.DMA
MESH = pl.DeviceIdType.MESH
PARTS = 8
HALF = ROWS // 2
MIB = 1024 * 1024


def vspec():
    return pl.BlockSpec(memory_space=pltpu.VMEM)


def dot(a, b):
    return jnp.dot(a, b, preferred_element_type=F32)


def iota(shape, dim):
    return lax.broadcasted_iota(jnp.int32, shape, dim)


def layer_norm(values):
    row_mean = jnp.mean(values, axis=-1, keepdims=True)
    centred = values - row_mean
    variance = jnp.mean(centred * centred, axis=-1, keepdims=True)
    return (centred * lax.rsqrt(variance + EPS)).astype(BF16)


def remote(source, target, send, recv, device):
    return pltpu.make_async_remote_copy(
        src_ref=source, dst_ref=target, send_sem=send, recv_sem=recv, device_id=device, device_id_type=MESH
    )


class Gather:
    def __init__(self, full, base, rows, split, send, recv, here):
        ctx, sess = here
        y, z_hi = ctx // 2, ctx % 2
        z_lo, x, core = sess // 8, (sess // 2) % 4, sess % 2
        z, odd = 2 * z_hi + z_lo, y % 2

        def device(x_at, y_at, z_at, core_at):
            return (2 * y_at + z_at // 2, (z_at % 2) * 8 + x_at * 2 + core_at)

        self.next, self.prev = device((x + 1) % 4, y, z, core), device((x + 3) % 4, y, z, core)
        self.above, self.below = device(x, y, (z + 1) % 4, core), device(x, y, (z + 3) % 4, core)
        self.front, self.back = device(x, (y + 1) % 4, z, core), device(x, (y + 3) % 4, z, core)
        self.twin = device(x, y, z, 1 - core)
        near = [x, (x + 3) % 4, (x + 1) % 4, (x + 2) % 4]
        mine = [near[0] * (1 - odd) + near[2] * odd, near[1] * (1 - odd) + near[3] * odd]
        theirs = [near[0] * odd + near[2] * (1 - odd), near[1] * odd + near[3] * (1 - odd)]
        at = lambda z_at, x_at, core_at: z_at * 8 + x_at * 2 + core_at
        self.own = sess
        self.a, self.b, self.c = (at(z_lo, i, core) for i in near[1:])
        self.give = [at(z_lo, i, core) for i in mine]
        self.take = [at(1 - z_lo, i, core) for i in mine]
        self.from_y = [at(1 - z_lo, i, core) for i in theirs]
        self.from_twin = (
            [at(z_lo, i, 1 - core) for i in near]
            + [at(1 - z_lo, i, 1 - core) for i in mine]
            + [at(1 - z_lo, i, 1 - core) for i in theirs]
        )
        self.other = [at(1 - z_lo, i, core) for i in near]
        self.twin_order = [at(z, i, 1 - core) for z in (z_lo, 1 - z_lo) for i in near]
        self.full = full
        self.all = pl.ds(base, rows)
        self.low, self.high = pl.ds(base, split), pl.ds(base + split, rows - split)
        self.send_sem, self.recv_sem = send, recv
        self.sent = []

    def copy(self, shard, rows, number, recv, device):
        part = self.full.at[shard, rows]
        return remote(part, part, self.send_sem.at[number], self.recv_sem.at[recv], device)

    def send(self, shard, rows, recv, device):
        what = (shard, rows, len(self.sent), recv, device)
        self.copy(*what).start()
        self.sent.append(what)

    def wait(self, shard, rows, recv):
        self.copy(shard, rows, 0, recv, self.twin).wait_recv()

    def start(self):
        self.send(self.own, self.all, 0, self.next)
        self.send(self.own, self.all, 1, self.prev)
        self.send(self.own, self.all, 12, self.twin)

    def along_x(self):
        self.wait(self.a, self.all, 0)
        self.send(self.a, self.low, 2, self.next)
        self.wait(self.b, self.all, 1)
        self.send(self.b, self.high, 3, self.prev)
        self.send(self.give[0], self.low, 4, self.above)
        self.send(self.give[0], self.high, 5, self.below)
        self.send(self.a, self.all, 13, self.twin)
        self.send(self.b, self.all, 14, self.twin)

    def across(self):
        self.wait(self.c, self.low, 2)
        self.wait(self.c, self.high, 3)
        self.send(self.give[1], self.low, 6, self.above)
        self.send(self.give[1], self.high, 7, self.below)
        self.send(self.c, self.all, 15, self.twin)

    def along_z(self, k):
        self.wait(self.take[k], self.low, 4 + 2 * k)
        self.send(self.take[k], self.low, 16 + 2 * k, self.front)
        self.wait(self.take[k], self.high, 5 + 2 * k)
        self.send(self.take[k], self.high, 17 + 2 * k, self.back)
        self.send(self.take[k], self.all, 8 + k, self.twin)

    def along_y(self):
        for k in range(2):
            self.wait(self.from_y[k], self.low, 16 + 2 * k)
            self.wait(self.from_y[k], self.high, 17 + 2 * k)
            self.send(self.from_y[k], self.all, 10 + k, self.twin)

    def finish(self):
        for shard, recv in zip(self.from_twin, (12, 13, 14, 15, 8, 9, 10, 11)):
            self.wait(shard, self.all, recv)

    def drain(self):
        for what in self.sent:
            self.copy(*what).wait_send()


class GatherAlongX(Gather):
    def begin(self):
        self.send(self.own, self.low, 0, self.above)
        self.send(self.own, self.high, 1, self.below)
        self.send(self.own, self.all, 10, self.twin)

    def start(self):
        self.send(self.own, self.all, 2, self.next)
        self.send(self.own, self.all, 3, self.prev)

    def start_other(self):
        z = self.other
        self.wait(z[0], self.low, 0)
        self.wait(z[0], self.high, 1)
        self.send(z[0], self.all, 4, self.next)
        self.send(z[0], self.all, 5, self.prev)
        self.send(z[0], self.all, 11, self.twin)

    def along_x(self, k):
        a, b = (self.a, self.b) if k == 0 else self.other[1:3]
        self.wait(a, self.all, 2 + 2 * k)
        self.send(a, self.low, 6 + 2 * k, self.next)
        self.wait(b, self.all, 3 + 2 * k)
        self.send(b, self.high, 7 + 2 * k, self.prev)
        self.send(a, self.all, 12 + 2 * k, self.twin)
        self.send(b, self.all, 13 + 2 * k, self.twin)

    def across(self, k):
        c = self.c if k == 0 else self.other[3]
        self.wait(c, self.low, 6 + 2 * k)
        self.wait(c, self.high, 7 + 2 * k)
        self.send(c, self.all, 16 + k, self.twin)

    def finish(self):
        for shard, recv in zip(self.twin_order, (10, 12, 13, 16, 11, 14, 15, 17)):
            self.wait(shard, self.all, recv)


GATHER_SENDS = 21
GATHER_RECVS = 20


def merged(block):
    return block.reshape(block.shape[0] * block.shape[1], block.shape[2])


def block_kernel(
    lengths, mel, route, first, second, kernel, lin_hbm, wq, wk, wv, wo, pw1,
    out, tail_full,
    mel_wide, high, low, slots, arrived, wide, turned, sorted_rows, frames, halo, last, sel, win_e, win_o,
    band, taps, even, odd, behind, sub, big, emb, normed, w_q, w_k, w_v, sent, held, context, heads, tail_own,
    residual, gated, edges, deep,
    mel_send, mel_recv, local_sem, halo_send, halo_recv,
    qkv_send, qkv_recv, head_send, head_recv, edge_send, edge_recv, gather_send, gather_recv,
):
    ctx, sess = lax.axis_index("ctx"), lax.axis_index("sess")
    me = ctx * 16 + sess
    total = ROWS + PAD
    here = (ctx, sess)
    after, before = ((ctx + 1) % PARTS, sess), ((ctx + PARTS - 1) % PARTS, sess)
    live_rows = lengths[sess] - ctx * ROWS

    barrier = pltpu.get_barrier_semaphore()

    def greet(i, carry):
        other = lax.rem(me + i, RANKS)
        pl.semaphore_signal(barrier, inc=1, device_id=(other // 16, other % 16), device_id_type=MESH)
        return carry

    lax.fori_loop(1, RANKS, greet, 0)
    own_copies = [
        pltpu.make_async_copy(source, target, local_sem.at[i])
        for i, (source, target) in enumerate(
            [
                (wk, w_k.at[sess]),
                (wv, w_v.at[sess]),
                (wq, w_q.at[sess]),
                (pw1.at[:, 0:D], tail_own.at[0:96]),
                (pw1.at[:, D : 2 * D], tail_own.at[96:192]),
                (wo, tail_own.at[192:240]),
                (lin_hbm, big),
            ]
        )
    ]
    for copy in own_copies:
        copy.start()
    lin_copy = own_copies[6]
    pack_slots(mel, route, mel_wide, high, low, wide, slots)
    own_slot = pltpu.make_async_copy(slots.at[me], arrived.at[me], local_sem.at[7])
    own_slot.start()
    prepare(first, second, sel, band, taps)
    gather_k, gather_v, gather_q, gather_t = (
        kind(full, base, rows, split, gather_send.at[i], gather_recv.at[i], here)
        for i, (kind, full, base, rows, split) in enumerate(
            [
                (Gather, w_k, 0, 96, 48),
                (Gather, w_v, 0, 96, 48),
                (Gather, w_q, 0, 96, 48),
                (GatherAlongX, tail_full, 0, 240, 128),
            ]
        )
    )
    for copy in own_copies[:6]:
        copy.wait()
    own_tail = pltpu.make_async_copy(tail_own, tail_full.at[sess], local_sem.at[3])
    own_tail.start()
    pl.semaphore_wait(barrier, RANKS - 1)
    gather_k.start()
    gather_v.start()
    gather_q.start()

    def deliver(i, carry):
        other = lax.rem(me + i, RANKS)
        remote(slots.at[other], arrived.at[me], mel_send, mel_recv, (other // 16, other % 16)).start()
        return carry

    lax.fori_loop(1, RANKS, deliver, 0)
    own_slot.wait()
    own_tail.wait()
    gather_t.begin()
    all_slots = remote(slots.at[0 : RANKS - 1], arrived.at[0 : RANKS - 1], mel_send, mel_recv, after)
    all_slots.wait_recv()

    place(me, arrived, wide, turned, sorted_rows, frames)
    halo_copy = remote(frames.at[ROWS - PAD :], halo, halo_send, halo_recv, after)
    halo_copy.start()
    gather_k.along_x()
    win_o[PAD:total, :] = dot(frames[:, 128:512], sel[...]).astype(BF16)
    halo_copy.wait_recv()
    first_rows = jnp.where(ctx > 0, halo[...].astype(F32), 0.0)
    last[0:PAD, :] = first_rows[:, 384:512]
    last[PAD:total, :] = frames[:, 384:512].astype(F32)
    previous = last[pl.ds(PAD - 1, ROWS), :].astype(BF16)
    win_e[...] = dot(jnp.concatenate([previous, frames[:, 0:256]], axis=1), sel[...]).astype(BF16)
    win_o[0:PAD, :] = dot(first_rows.astype(BF16)[:, 128:512], sel[...]).astype(BF16)
    gather_v.along_x()

    plan = [
        [gather_k.across, lambda: gather_k.along_z(0), gather_q.along_x],
        [gather_v.across, lambda: gather_v.along_z(0), gather_t.start],
        [gather_q.across, lambda: gather_q.along_z(0), lambda: gather_k.along_z(1)],
        [lambda: gather_v.along_z(1), gather_t.start_other],
        [lambda: gather_q.along_z(1), gather_k.along_y],
        [gather_v.along_y],
        [gather_q.along_y],
        [gather_k.finish, gather_v.finish],
    ]

    def four_bins(g, side):
        q = pl.ds(pl.multiple_of((g // 4) * 128, 128), 128)
        weights = band[:, pl.ds(pl.multiple_of((g % 4) * 512, 512), 512)]
        even[side, :, 128:640] = jnp.maximum(dot(win_e[:, q], weights), 0.0).astype(BF16)
        odd[side, :, 128:640] = jnp.maximum(dot(win_o[:, q], weights), 0.0).astype(BF16)
        even[1 - side, :, 0:128] = even[side, :, 512:640]
        odd[1 - side, :, 0:128] = odd[side, :, 512:640]

    def two_bins(g, side):
        behind[...] = dot(odd[side], taps[1280:1920, :])
        both = jnp.concatenate([even[side], odd[side, PAD:, :]], axis=1)
        rows = dot(both, taps[0:1280, :]) + behind[pl.ds(PAD - 1, ROWS), :]
        sub[:, pl.ds(pl.multiple_of(g * 256, 256), 256)] = jnp.maximum(rows, 0.0).astype(BF16)

    def groups(i, carry):
        four_bins(2 * i, 0)
        two_bins(2 * i, 0)
        four_bins(2 * i + 1, 1)
        two_bins(2 * i + 1, 1)
        for step, actions in enumerate(plan):

            @pl.when(i == step)
            def _():
                for action in actions:
                    action()

        return carry

    even[0, :, 0:128] = jnp.zeros((ROWS, 128), BF16)
    odd[0, :, 0:128] = jnp.zeros((total, 128), BF16)
    lax.fori_loop(0, 8, groups, 0)
    lin_copy.wait()

    def rows_of(half, carry):
        start = pl.multiple_of(half * HALF, HALF)
        mine = pl.ds(start, HALF)

        def project(n, carry):
            at = pl.ds(pl.multiple_of(n * 512, 512), 512)
            emb[mine, at] = dot(sub[mine, :], merged(big[:, :, at])).astype(BF16)
            return carry

        lax.fori_loop(0, 3, project, 0)
        normed[mine, :] = layer_norm(emb[mine, :].astype(F32))

        @pl.when(half == 0)
        def _():
            gather_q.finish()

        lane = iota((HALF, 128), 1)
        live = iota((HALF, 128), 0) < live_rows - start
        for part, weights in ((1, w_k), (2, w_v), (0, w_q)):
            rows = dot(normed[mine, :], merged(weights[...]))
            if part == 1:
                extra = jnp.where(live, 0.0, -1e30)
            else:
                extra = jnp.ones((HALF, 128), F32)
            for h in range(HEADS):
                base, shift = (96 * h) // 128 * 128, (96 * h) % 128
                if shift == 0:
                    head = rows[:, base : base + 128]
                elif shift == 32:
                    head = pltpu.roll(rows[:, base : base + 128], 128 - shift, 1)
                else:
                    head = pltpu.roll(rows[:, base : base + 256], 256 - shift, 1)[:, 0:128]
                head = jnp.where(lane < HEAD, head, jnp.where(lane == HEAD, extra, 0.0))
                sent[part, h, mine] = head.astype(BF16)
            own_share(half, part).start()

            def share(i, carry):
                share_of(half, part, i).start()
                return carry

            lax.fori_loop(1, PARTS, share, 0)
        return carry

    def own_share(half, part):
        mine = pl.ds(pl.multiple_of(half * HALF, HALF), HALF)
        return pltpu.make_async_copy(
            sent.at[part, ctx, mine], held.at[part, ctx, mine], local_sem.at[8 + 3 * half + part]
        )

    def share_of(half, part, i):
        mine = pl.ds(pl.multiple_of(half * HALF, HALF), HALF)
        other = lax.rem(ctx + i, PARTS)
        return remote(
            sent.at[part, other, mine], held.at[part, ctx, mine],
            qkv_send.at[half, part, i], qkv_recv.at[half, part, i], (other, sess),
        )

    lax.fori_loop(0, 2, rows_of, 0)
    gather_t.along_x(0)
    for half in range(2):
        for part in range(3):
            own_share(half, part).wait()
    for part in (1, 2):
        for half in range(2):

            def arrive(i, carry):
                share_of(half, part, i).wait_recv()
                return carry

            lax.fori_loop(1, PARTS, arrive, 0)

    scale = math.log2(math.e) / math.sqrt(HEAD)

    def attend(i):
        other = lax.rem(ctx + PARTS - i, PARTS)
        keys, values = merged(held[1]), merged(held[2])
        for half in range(2):
            at = pl.ds(half * HALF, HALF)
            scores = lax.dot_general(
                held[0, other, at, :], keys, (((1,), (1,)), ((), ())), preferred_element_type=F32
            )
            row_max = jnp.max(scores, axis=1, keepdims=True)
            weights = jnp.exp2((scores - row_max) * scale).astype(BF16)
            summed = dot(weights, values)
            result = summed / summed[:, HEAD : HEAD + 1]
            result = jnp.where(iota(result.shape, 1) < HEAD, result, 0.0)
            context[other, at, :] = result.astype(BF16)

    def head_of(i):
        other = lax.rem(ctx + PARTS - i, PARTS)
        return remote(
            context.at[other], heads.at[ctx], head_send.at[i], head_recv.at[i], (other, sess)
        )

    later = {
        3: [lambda: gather_t.along_x(1)],
        4: [lambda: gather_t.across(0)],
        7: [lambda: gather_t.across(1), gather_t.finish],
    }
    tail_copy = pltpu.make_async_copy(tail_full, big.at[:, 0:240, :], local_sem.at[14])
    later[7].append(tail_copy.start)

    def attend_for(i, carry):
        @pl.when(i < PARTS)
        def _():
            share_of(0, 0, i).wait_recv()
            share_of(1, 0, i).wait_recv()

        attend(i)

        @pl.when(i < PARTS)
        def _():
            head_of(i).start()

        for at, actions in later.items():

            @pl.when(i == at)
            def _():
                for action in actions:
                    action()

        return carry

    lax.fori_loop(1, PARTS + 1, attend_for, 0)
    own_head = pltpu.make_async_copy(context.at[ctx], heads.at[ctx], local_sem.at[15])
    own_head.start()
    own_head.wait()

    def arrive_heads(i, carry):
        head_of(i).wait()
        return carry

    lax.fori_loop(1, PARTS, arrive_heads, 0)
    tail_copy.wait()

    w_out = merged(big[:, 192:240, :])
    summed = emb[...].astype(F32)
    for pair in range(4):
        left = jnp.concatenate([heads[2 * pair], heads[2 * pair + 1]], axis=1)
        at = 192 * pair
        pad = jnp.zeros((32, D), BF16)
        right = jnp.concatenate([w_out[at : at + 96], pad, w_out[at + 96 : at + 192], pad], axis=0)
        summed = summed + dot(left, right)
    residual[...] = summed.astype(BF16)
    normed[...] = layer_norm(residual[...].astype(F32))
    live = iota((ROWS, 256), 0) < live_rows

    def lift(n, carry):
        at = pl.ds(pl.multiple_of(n * 256, 256), 256)
        value = dot(normed[...], merged(big[:, 0:96, at]))
        gate = dot(normed[...], merged(big[:, 96:192, at]))
        rows = jnp.where(live, value * jax.nn.sigmoid(gate), 0.0).astype(BF16)
        gated[:, at] = rows
        wide_rows = rows.astype(F32)
        deep[2 * n, PAD : PAD + ROWS, :] = wide_rows[:, 0:128]
        deep[2 * n + 1, PAD : PAD + ROWS, :] = wide_rows[:, 128:256]
        return carry

    lax.fori_loop(0, 6, lift, 0)
    to_after = remote(gated.at[ROWS - PAD :], edges.at[0], edge_send.at[0], edge_recv.at[0], after)
    to_before = remote(gated.at[0:PAD], edges.at[1], edge_send.at[1], edge_recv.at[1], before)
    to_after.start()
    to_before.start()

    def taps_of(n, starts):
        at = pl.ds(pl.multiple_of(n * 128, 128), 128)
        weights = kernel[:, at].astype(F32)
        for start in starts:
            rows = jnp.zeros((64, 128), F32)
            for j in range(KERNEL):
                rows = rows + deep[n, pl.ds(start + j + 1, 64), :] * weights[j : j + 1, :]
            rows = residual[start : start + 64, at].astype(F32) + rows * jax.nn.sigmoid(rows)
            out[start : start + 64, at] = rows.astype(BF16)

    def inner(n, carry):
        taps_of(n, (64, 128, 192, 256))
        return carry

    def outer(n, carry):
        at = pl.ds(pl.multiple_of(n * 128, 128), 128)
        deep[n, 0:PAD, :] = jnp.where(ctx > 0, edges[0, :, at].astype(F32), 0.0)
        deep[n, PAD + ROWS :, :] = jnp.where(ctx < PARTS - 1, edges[1, :, at].astype(F32), 0.0)
        taps_of(n, (0, 320))
        return carry

    lax.fori_loop(0, D // 128, inner, 0)
    to_after.wait_recv()
    to_before.wait_recv()
    lax.fori_loop(0, D // 128, outer, 0)

    all_slots.wait_send()
    halo_copy.wait_send()
    to_after.wait_send()
    to_before.wait_send()
    for half in range(2):
        for part in range(3):

            def leave(i, carry):
                share_of(half, part, i).wait_send()
                return carry

            lax.fori_loop(1, PARTS, leave, 0)
    for gather in (gather_k, gather_v, gather_q, gather_t):
        gather.drain()


def pack_slots(mel, route, mel_wide, high, low, wide, slots):
    mel_wide[...] = mel[...].astype(F32)
    high[...] = jnp.zeros_like(high)
    low[...] = jnp.zeros_like(low)
    high[0:SLOT, :] = (route[...] // 64).astype(F32)
    low[0:SLOT, :] = (route[...] % 64).astype(F32)

    def fill(j, carry):
        to = pl.multiple_of(16 * j, 16)
        at = (SLOT * j) // 128
        wide[pl.ds(to, SLOT), :] = mel_wide[pl.ds(SLOT * j, SLOT), :]
        wide[pl.ds(to + SLOT, 2), :] = high[pl.ds(at, 2), :]
        wide[pl.ds(to + SLOT + 2, 2), :] = low[pl.ds(at, 2), :]
        return carry

    lax.fori_loop(0, RANKS, fill, 0, unroll=8)
    slots[...] = wide[...].astype(BF16).reshape(RANKS, 16, 128)


def prepare(first, second, sel, band, taps):
    row = iota((384, 512), 0)
    col = iota((384, 512), 1)
    a, m, p, r = row // 128, row % 128, col // 32, col % 32
    b = jnp.where(r >= 9, 1, 0) + jnp.where(r >= 18, 1, 0)
    hit = (r < 27) & (a == b) & (m == 8 * p - 1 + r - 9 * b)
    sel[...] = jnp.where(hit, 1.0, 0.0).astype(BF16)
    band_row = iota((128, 128), 0)
    values = first[...].astype(F32)
    for f in range(16):
        block = jnp.zeros((128, 128), F32)
        for tap in range(9):
            at = 32 * (f // 4) + 9 * (tap // 3) + 2 * (f % 4) + tap % 3
            block = jnp.where(band_row == at, values[tap : tap + 1, :], block)
        band[:, 128 * f : 128 * (f + 1)] = block.astype(BF16)
    taps[...] = jnp.zeros_like(taps)
    for position, row_tap in enumerate((1, 2, 0)):
        for o in range(2):
            for c in range(3):
                at = 640 * position + 128 * (2 * o + c)
                source = (3 * row_tap + c) * 128
                taps[at : at + 128, 128 * o : 128 * (o + 1)] = second[source : source + 128, :]


def place(me, arrived, wide, turned, sorted_rows, frames):
    wide[...] = merged(arrived[...]).astype(F32)
    for k in range(2):
        high = wide[pl.ds(SLOT + k, RANKS, stride=16), :]
        low = wide[pl.ds(SLOT + 2 + k, RANKS, stride=16), :]
        turned[128 * k : 128 * (k + 1), :] = (high * 64.0 + low).T
    position = turned[pl.ds((SLOT * me) % 128, SLOT), :]
    for r in range(SLOT):
        sorted_rows[r * RANKS : (r + 1) * RANKS, :] = wide[pl.ds(r, RANKS, stride=16), :].astype(BF16)
    target = iota((ROWS, RANKS), 0).astype(F32) * 4.0
    for k in range(4):
        chosen = jnp.concatenate(
            [
                jnp.where(position[r : r + 1, :] == target + float(k), 1.0, 0.0).astype(BF16)
                for r in range(SLOT)
            ],
            axis=1,
        )
        frames[:, 128 * k : 128 * (k + 1)] = dot(chosen, sorted_rows[...]).astype(BF16)


def block(lengths, mel, route, first, second, kernel, lin_in, wq, wk, wv, wo, pw1):
    total = ROWS + PAD
    anywhere = pl.BlockSpec(memory_space=pl.ANY)
    return pl.pallas_call(
        block_kernel,
        out_shape=[
            jax.ShapeDtypeStruct((ROWS, D), BF16),
            jax.ShapeDtypeStruct((16, 240, D), BF16),
        ],
        in_specs=[pl.BlockSpec(memory_space=pltpu.SMEM)] + [vspec()] * 5 + [anywhere] * 6,
        out_specs=[vspec(), anywhere],
        scratch_shapes=[
            VMEM((RANKS * SLOT, 128), F32),
            VMEM((16, 128), F32),
            VMEM((16, 128), F32),
            VMEM((RANKS, 16, 128), BF16),
            VMEM((RANKS, 16, 128), BF16),
            VMEM((16 * RANKS, 128), F32),
            VMEM((256, 128), F32),
            VMEM((SLOT * RANKS, 128), BF16),
            VMEM((ROWS, 512), BF16),
            VMEM((PAD, 512), BF16),
            VMEM((total, 128), F32),
            VMEM((384, 512), BF16),
            VMEM((ROWS, 512), BF16),
            VMEM((total, 512), BF16),
            VMEM((128, 2048), BF16),
            VMEM((1920, 256), BF16),
            VMEM((2, ROWS, 640), BF16),
            VMEM((2, total, 640), BF16),
            VMEM((total, 256), F32),
            VMEM((ROWS, 4096), BF16),
            VMEM((16, 256, D), BF16),
            VMEM((ROWS, D), BF16),
            VMEM((ROWS, D), BF16),
            VMEM((16, 96, 768), BF16),
            VMEM((16, 96, 768), BF16),
            VMEM((16, 96, 768), BF16),
            VMEM((3, HEADS, ROWS, 128), BF16),
            VMEM((3, HEADS, ROWS, 128), BF16),
            VMEM((HEADS, ROWS, 128), BF16),
            VMEM((HEADS, ROWS, 128), BF16),
            VMEM((240, D), BF16),
            VMEM((ROWS, D), BF16),
            VMEM((ROWS, D), BF16),
            VMEM((2, PAD, D), BF16),
            VMEM((D // 128, ROWS + 2 * PAD, 128), F32),
            DMA, DMA, DMA((16,)), DMA, DMA,
            DMA((2, 3, PARTS)), DMA((2, 3, PARTS)), DMA((PARTS,)), DMA((PARTS,)), DMA((2,)), DMA((2,)),
            DMA((4, GATHER_SENDS)), DMA((4, GATHER_RECVS)),
        ],
        compiler_params=pltpu.CompilerParams(
            vmem_limit_bytes=62 * MIB, collective_id=0, has_side_effects=True
        ),
        cost_estimate=pl.CostEstimate(
            flops=27_000_000_000, bytes_accessed=60_000_000, transcendentals=12_000_000
        ),
        name="conformer_block",
    )(lengths, mel, route, first, second, kernel, lin_in, wq, wk, wv, wo, pw1)


def local(mel_in, route, lengths, conv_first, conv_second, lin_in, wq, wk, wv, wo, pw1, dw_kernel):
    encoded, _ = block(
        lengths, mel_in, route.reshape(SLOT, 128), conv_first, conv_second, dw_kernel,
        lin_in.reshape(16, 256, D), wq, wk, wv, wo, pw1,
    )
    return encoded[None]


def solution(mesh):
    return jax.shard_map(
        local,
        mesh=mesh,
        in_specs=(
            P(("ctx", "sess"), None),
            P(("ctx", "sess")),
            P(),
            P(),
            P(),
            P(),
            P("sess", None),
            P("sess", None),
            P("sess", None),
            P("sess", None),
            P("sess", None),
            P(),
        ),
        out_specs=P("sess", "ctx", None),
        check_vma=False,
    )
```

```python
import functools
import math

import jax
import jax.numpy as jnp
from jax import lax
from jax.experimental import pallas as pl
from jax.experimental.pallas import tpu as pltpu
from jax.sharding import PartitionSpec as P

HEADS = 8
HEAD = 96
KERNEL = 31
EPS = 1e-05
ROWS = 384
PAD = 16
SLOT = 12
RANKS = 128
D = 1536
F32 = jnp.float32
BF16 = jnp.bfloat16
VMEM = pltpu.VMEM
DMA = pltpu.SemaphoreType.DMA
MESH = pl.DeviceIdType.MESH
PARTS = 8
HALF = ROWS // 2
MIB = 1024 * 1024


def vspec():
    return pl.BlockSpec(memory_space=pltpu.VMEM)


def dot(a, b):
    return jnp.dot(a, b, preferred_element_type=F32)


def iota(shape, dim):
    return lax.broadcasted_iota(jnp.int32, shape, dim)


def layer_norm(values):
    row_mean = jnp.mean(values, axis=-1, keepdims=True)
    centred = values - row_mean
    variance = jnp.mean(centred * centred, axis=-1, keepdims=True)
    return (centred * lax.rsqrt(variance + EPS)).astype(BF16)


def remote(source, target, send, recv, device):
    return pltpu.make_async_remote_copy(
        src_ref=source, dst_ref=target, send_sem=send, recv_sem=recv, device_id=device, device_id_type=MESH
    )


class Gather:
    def __init__(self, full, base, rows, split, send, recv, here):
        ctx, sess = here
        y, z_hi = ctx // 2, ctx % 2
        z_lo, x, core = sess // 8, (sess // 2) % 4, sess % 2
        z, odd = 2 * z_hi + z_lo, y % 2

        def device(x_at, y_at, z_at, core_at):
            return (2 * y_at + z_at // 2, (z_at % 2) * 8 + x_at * 2 + core_at)

        self.next, self.prev = device((x + 1) % 4, y, z, core), device((x + 3) % 4, y, z, core)
        self.above, self.below = device(x, y, (z + 1) % 4, core), device(x, y, (z + 3) % 4, core)
        self.front, self.back = device(x, (y + 1) % 4, z, core), device(x, (y + 3) % 4, z, core)
        self.twin = device(x, y, z, 1 - core)
        near = [x, (x + 3) % 4, (x + 1) % 4, (x + 2) % 4]
        mine = [near[0] * (1 - odd) + near[2] * odd, near[1] * (1 - odd) + near[3] * odd]
        theirs = [near[0] * odd + near[2] * (1 - odd), near[1] * odd + near[3] * (1 - odd)]
        at = lambda z_at, x_at, core_at: z_at * 8 + x_at * 2 + core_at
        self.own = sess
        self.a, self.b, self.c = (at(z_lo, i, core) for i in near[1:])
        self.give = [at(z_lo, i, core) for i in mine]
        self.take = [at(1 - z_lo, i, core) for i in mine]
        self.from_y = [at(1 - z_lo, i, core) for i in theirs]
        self.from_twin = (
            [at(z_lo, i, 1 - core) for i in near]
            + [at(1 - z_lo, i, 1 - core) for i in mine]
            + [at(1 - z_lo, i, 1 - core) for i in theirs]
        )
        self.other = [at(1 - z_lo, i, core) for i in near]
        self.twin_order = [at(z, i, 1 - core) for z in (z_lo, 1 - z_lo) for i in near]
        self.full = full
        self.all = pl.ds(base, rows)
        self.low, self.high = pl.ds(base, split), pl.ds(base + split, rows - split)
        self.send_sem, self.recv_sem = send, recv
        self.sent = []

    def copy(self, shard, rows, number, recv, device):
        part = self.full.at[shard, rows]
        return remote(part, part, self.send_sem.at[number], self.recv_sem.at[recv], device)

    def send(self, shard, rows, recv, device):
        what = (shard, rows, len(self.sent), recv, device)
        self.copy(*what).start()
        self.sent.append(what)

    def wait(self, shard, rows, recv):
        self.copy(shard, rows, 0, recv, self.twin).wait_recv()

    def start(self):
        self.send(self.own, self.all, 0, self.next)
        self.send(self.own, self.all, 1, self.prev)
        self.send(self.own, self.all, 12, self.twin)

    def along_x(self):
        self.wait(self.a, self.all, 0)
        self.send(self.a, self.low, 2, self.next)
        self.wait(self.b, self.all, 1)
        self.send(self.b, self.high, 3, self.prev)
        self.send(self.give[0], self.low, 4, self.above)
        self.send(self.give[0], self.high, 5, self.below)
        self.send(self.a, self.all, 13, self.twin)
        self.send(self.b, self.all, 14, self.twin)

    def across(self):
        self.wait(self.c, self.low, 2)
        self.wait(self.c, self.high, 3)
        self.send(self.give[1], self.low, 6, self.above)
        self.send(self.give[1], self.high, 7, self.below)
        self.send(self.c, self.all, 15, self.twin)

    def along_z(self, k):
        self.wait(self.take[k], self.low, 4 + 2 * k)
        self.send(self.take[k], self.low, 16 + 2 * k, self.front)
        self.wait(self.take[k], self.high, 5 + 2 * k)
        self.send(self.take[k], self.high, 17 + 2 * k, self.back)
        self.send(self.take[k], self.all, 8 + k, self.twin)

    def along_y(self):
        for k in range(2):
            self.wait(self.from_y[k], self.low, 16 + 2 * k)
            self.wait(self.from_y[k], self.high, 17 + 2 * k)
            self.send(self.from_y[k], self.all, 10 + k, self.twin)

    def finish(self):
        for shard, recv in zip(self.from_twin, (12, 13, 14, 15, 8, 9, 10, 11)):
            self.wait(shard, self.all, recv)

    def drain(self):
        for what in self.sent:
            self.copy(*what).wait_send()


class GatherAlongX(Gather):
    def begin(self):
        self.send(self.own, self.low, 0, self.above)
        self.send(self.own, self.high, 1, self.below)
        self.send(self.own, self.all, 10, self.twin)

    def start(self):
        self.send(self.own, self.all, 2, self.next)
        self.send(self.own, self.all, 3, self.prev)

    def start_other(self):
        z = self.other
        self.wait(z[0], self.low, 0)
        self.wait(z[0], self.high, 1)
        self.send(z[0], self.all, 4, self.next)
        self.send(z[0], self.all, 5, self.prev)
        self.send(z[0], self.all, 11, self.twin)

    def along_x(self, k):
        a, b = (self.a, self.b) if k == 0 else self.other[1:3]
        self.wait(a, self.all, 2 + 2 * k)
        self.send(a, self.low, 6 + 2 * k, self.next)
        self.wait(b, self.all, 3 + 2 * k)
        self.send(b, self.high, 7 + 2 * k, self.prev)
        self.send(a, self.all, 12 + 2 * k, self.twin)
        self.send(b, self.all, 13 + 2 * k, self.twin)

    def across(self, k):
        c = self.c if k == 0 else self.other[3]
        self.wait(c, self.low, 6 + 2 * k)
        self.wait(c, self.high, 7 + 2 * k)
        self.send(c, self.all, 16 + k, self.twin)

    def finish(self):
        for shard, recv in zip(self.twin_order, (10, 12, 13, 16, 11, 14, 15, 17)):
            self.wait(shard, self.all, recv)


GATHER_SENDS = 21
GATHER_RECVS = 20


def merged(block):
    return block.reshape(block.shape[0] * block.shape[1], block.shape[2])


def block_kernel(
    lengths, mel, route, first, second, kernel, lin_hbm, wq, wk, wv, wo, pw1,
    out, tail_full,
    mel_wide, high, low, slots, arrived, wide, turned, sorted_rows, frames, halo, last, sel, win_e, win_o,
    band, taps, even, odd, behind, sub, big, emb, normed, w_q, w_k, w_v, sent, held, context, heads, tail_own,
    residual, gated, edges, deep,
    mel_send, mel_recv, local_sem, halo_send, halo_recv,
    qkv_send, qkv_recv, head_send, head_recv, edge_send, edge_recv, gather_send, gather_recv,
):
    ctx, sess = lax.axis_index("ctx"), lax.axis_index("sess")
    me = ctx * 16 + sess
    total = ROWS + PAD
    here = (ctx, sess)
    after, before = ((ctx + 1) % PARTS, sess), ((ctx + PARTS - 1) % PARTS, sess)
    live_rows = lengths[sess] - ctx * ROWS

    barrier = pltpu.get_barrier_semaphore()

    def greet(i, carry):
        other = lax.rem(me + i, RANKS)
        pl.semaphore_signal(barrier, inc=1, device_id=(other // 16, other % 16), device_id_type=MESH)
        return carry

    lax.fori_loop(1, RANKS, greet, 0)
    own_copies = [
        pltpu.make_async_copy(source, target, local_sem.at[i])
        for i, (source, target) in enumerate(
            [
                (wk, w_k.at[sess]),
                (wv, w_v.at[sess]),
                (wq, w_q.at[sess]),
                (pw1.at[:, 0:D], tail_own.at[0:96]),
                (pw1.at[:, D : 2 * D], tail_own.at[96:192]),
                (wo, tail_own.at[192:240]),
                (lin_hbm, big),
            ]
        )
    ]
    for copy in own_copies:
        copy.start()
    lin_copy = own_copies[6]
    pack_slots(mel, route, mel_wide, high, low, wide, slots)
    own_slot = pltpu.make_async_copy(slots.at[me], arrived.at[me], local_sem.at[7])
    own_slot.start()
    prepare(first, second, sel, band, taps)
    gather_k, gather_v, gather_q, gather_t = (
        kind(full, base, rows, split, gather_send.at[i], gather_recv.at[i], here)
        for i, (kind, full, base, rows, split) in enumerate(
            [
                (Gather, w_k, 0, 96, 48),
                (Gather, w_v, 0, 96, 48),
                (Gather, w_q, 0, 96, 48),
                (GatherAlongX, tail_full, 0, 240, 128),
            ]
        )
    )
    for copy in own_copies[:6]:
        copy.wait()
    own_tail = pltpu.make_async_copy(tail_own, tail_full.at[sess], local_sem.at[3])
    own_tail.start()
    pl.semaphore_wait(barrier, RANKS - 1)

    def deliver(i, carry):
        other = lax.rem(me + i, RANKS)
        remote(slots.at[other], arrived.at[me], mel_send, mel_recv, (other // 16, other % 16)).start()
        return carry

    lax.fori_loop(1, RANKS, deliver, 0)
    gather_k.start()
    gather_v.start()
    gather_q.start()
    own_slot.wait()
    own_tail.wait()
    gather_t.begin()
    all_slots = remote(slots.at[0 : RANKS - 1], arrived.at[0 : RANKS - 1], mel_send, mel_recv, after)
    all_slots.wait_recv()

    place(me, arrived, wide, turned, sorted_rows, frames)
    halo_copy = remote(frames.at[ROWS - PAD :], halo, halo_send, halo_recv, after)
    halo_copy.start()
    gather_k.along_x()
    win_o[PAD:total, :] = dot(frames[:, 128:512], sel[...]).astype(BF16)
    halo_copy.wait_recv()
    first_rows = jnp.where(ctx > 0, halo[...].astype(F32), 0.0)
    last[0:PAD, :] = first_rows[:, 384:512]
    last[PAD:total, :] = frames[:, 384:512].astype(F32)
    previous = last[pl.ds(PAD - 1, ROWS), :].astype(BF16)
    win_e[...] = dot(jnp.concatenate([previous, frames[:, 0:256]], axis=1), sel[...]).astype(BF16)
    win_o[0:PAD, :] = dot(first_rows.astype(BF16)[:, 128:512], sel[...]).astype(BF16)
    gather_v.along_x()

    plan = [
        [gather_k.across, lambda: gather_k.along_z(0), gather_q.along_x],
        [gather_v.across, lambda: gather_v.along_z(0), gather_t.start],
        [gather_q.across, lambda: gather_q.along_z(0), lambda: gather_k.along_z(1)],
        [lambda: gather_v.along_z(1), gather_t.start_other],
        [lambda: gather_q.along_z(1), gather_k.along_y],
        [gather_v.along_y],
        [gather_q.along_y],
        [gather_k.finish, gather_v.finish],
    ]

    def four_bins(g, side):
        q = pl.ds(pl.multiple_of((g // 4) * 128, 128), 128)
        weights = band[:, pl.ds(pl.multiple_of((g % 4) * 512, 512), 512)]
        even[side, :, 128:640] = jnp.maximum(dot(win_e[:, q], weights), 0.0).astype(BF16)
        odd[side, :, 128:640] = jnp.maximum(dot(win_o[:, q], weights), 0.0).astype(BF16)
        even[1 - side, :, 0:128] = even[side, :, 512:640]
        odd[1 - side, :, 0:128] = odd[side, :, 512:640]

    def two_bins(g, side):
        behind[...] = dot(odd[side], taps[1280:1920, :])
        both = jnp.concatenate([even[side], odd[side, PAD:, :]], axis=1)
        rows = dot(both, taps[0:1280, :]) + behind[pl.ds(PAD - 1, ROWS), :]
        sub[:, pl.ds(pl.multiple_of(g * 256, 256), 256)] = jnp.maximum(rows, 0.0).astype(BF16)

    def groups(i, carry):
        four_bins(2 * i, 0)
        two_bins(2 * i, 0)
        four_bins(2 * i + 1, 1)
        two_bins(2 * i + 1, 1)
        for step, actions in enumerate(plan):

            @pl.when(i == step)
            def _():
                for action in actions:
                    action()

        return carry

    even[0, :, 0:128] = jnp.zeros((ROWS, 128), BF16)
    odd[0, :, 0:128] = jnp.zeros((total, 128), BF16)
    lax.fori_loop(0, 8, groups, 0)
    lin_copy.wait()

    def rows_of(half, carry):
        start = pl.multiple_of(half * HALF, HALF)
        mine = pl.ds(start, HALF)

        def project(n, carry):
            at = pl.ds(pl.multiple_of(n * 512, 512), 512)
            emb[mine, at] = dot(sub[mine, :], merged(big[:, :, at])).astype(BF16)
            return carry

        lax.fori_loop(0, 3, project, 0)
        normed[mine, :] = layer_norm(emb[mine, :].astype(F32))

        @pl.when(half == 0)
        def _():
            gather_q.finish()

        lane = iota((HALF, 128), 1)
        live = iota((HALF, 128), 0) < live_rows - start
        for part, weights in ((1, w_k), (2, w_v), (0, w_q)):
            rows = dot(normed[mine, :], merged(weights[...]))
            if part == 1:
                extra = jnp.where(live, 0.0, -1e30)
            else:
                extra = jnp.ones((HALF, 128), F32)
            for h in range(HEADS):
                base, shift = (96 * h) // 128 * 128, (96 * h) % 128
                if shift == 0:
                    head = rows[:, base : base + 128]
                elif shift == 32:
                    head = pltpu.roll(rows[:, base : base + 128], 128 - shift, 1)
                else:
                    head = pltpu.roll(rows[:, base : base + 256], 256 - shift, 1)[:, 0:128]
                head = jnp.where(lane < HEAD, head, jnp.where(lane == HEAD, extra, 0.0))
                sent[part, h, mine] = head.astype(BF16)
            own_share(half, part).start()

            def share(i, carry):
                share_of(half, part, i).start()
                return carry

            lax.fori_loop(1, PARTS, share, 0)
        return carry

    def own_share(half, part):
        mine = pl.ds(pl.multiple_of(half * HALF, HALF), HALF)
        return pltpu.make_async_copy(
            sent.at[part, ctx, mine], held.at[part, ctx, mine], local_sem.at[8 + 3 * half + part]
        )

    def share_of(half, part, i):
        mine = pl.ds(pl.multiple_of(half * HALF, HALF), HALF)
        other = lax.rem(ctx + i, PARTS)
        return remote(
            sent.at[part, other, mine], held.at[part, ctx, mine],
            qkv_send.at[half, part, i], qkv_recv.at[half, part, i], (other, sess),
        )

    lax.fori_loop(0, 2, rows_of, 0)
    gather_t.along_x(0)
    for half in range(2):
        for part in range(3):
            own_share(half, part).wait()
    for part in (1, 2):
        for half in range(2):

            def arrive(i, carry):
                share_of(half, part, i).wait_recv()
                return carry

            lax.fori_loop(1, PARTS, arrive, 0)

    scale = math.log2(math.e) / math.sqrt(HEAD)

    def attend(i):
        other = lax.rem(ctx + PARTS - i, PARTS)
        keys, values = merged(held[1]), merged(held[2])
        for half in range(2):
            at = pl.ds(half * HALF, HALF)
            scores = lax.dot_general(
                held[0, other, at, :], keys, (((1,), (1,)), ((), ())), preferred_element_type=F32
            )
            row_max = jnp.max(scores, axis=1, keepdims=True)
            weights = jnp.exp2((scores - row_max) * scale).astype(BF16)
            summed = dot(weights, values)
            result = summed / summed[:, HEAD : HEAD + 1]
            result = jnp.where(iota(result.shape, 1) < HEAD, result, 0.0)
            context[other, at, :] = result.astype(BF16)

    def head_of(i):
        other = lax.rem(ctx + PARTS - i, PARTS)
        return remote(
            context.at[other], heads.at[ctx], head_send.at[i], head_recv.at[i], (other, sess)
        )

    later = {
        3: [lambda: gather_t.along_x(1)],
        4: [lambda: gather_t.across(0)],
        7: [lambda: gather_t.across(1), gather_t.finish],
    }
    tail_copy = pltpu.make_async_copy(tail_full, big.at[:, 0:240, :], local_sem.at[14])
    later[7].append(tail_copy.start)

    def attend_for(i, carry):
        @pl.when(i < PARTS)
        def _():
            share_of(0, 0, i).wait_recv()
            share_of(1, 0, i).wait_recv()

        attend(i)

        @pl.when(i < PARTS)
        def _():
            head_of(i).start()

        for at, actions in later.items():

            @pl.when(i == at)
            def _():
                for action in actions:
                    action()

        return carry

    lax.fori_loop(1, PARTS + 1, attend_for, 0)
    own_head = pltpu.make_async_copy(context.at[ctx], heads.at[ctx], local_sem.at[15])
    own_head.start()
    own_head.wait()

    def arrive_heads(i, carry):
        head_of(i).wait()
        return carry

    lax.fori_loop(1, PARTS, arrive_heads, 0)
    tail_copy.wait()

    w_out = merged(big[:, 192:240, :])
    summed = emb[...].astype(F32)
    for pair in range(4):
        left = jnp.concatenate([heads[2 * pair], heads[2 * pair + 1]], axis=1)
        at = 192 * pair
        pad = jnp.zeros((32, D), BF16)
        right = jnp.concatenate([w_out[at : at + 96], pad, w_out[at + 96 : at + 192], pad], axis=0)
        summed = summed + dot(left, right)
    residual[...] = summed.astype(BF16)
    normed[...] = layer_norm(residual[...].astype(F32))
    live = iota((ROWS, 256), 0) < live_rows

    def lift(n, carry):
        at = pl.ds(pl.multiple_of(n * 256, 256), 256)
        value = dot(normed[...], merged(big[:, 0:96, at]))
        gate = dot(normed[...], merged(big[:, 96:192, at]))
        rows = jnp.where(live, value * jax.nn.sigmoid(gate), 0.0).astype(BF16)
        gated[:, at] = rows
        wide_rows = rows.astype(F32)
        deep[2 * n, PAD : PAD + ROWS, :] = wide_rows[:, 0:128]
        deep[2 * n + 1, PAD : PAD + ROWS, :] = wide_rows[:, 128:256]
        return carry

    lax.fori_loop(0, 6, lift, 0)
    to_after = remote(gated.at[ROWS - PAD :], edges.at[0], edge_send.at[0], edge_recv.at[0], after)
    to_before = remote(gated.at[0:PAD], edges.at[1], edge_send.at[1], edge_recv.at[1], before)
    to_after.start()
    to_before.start()

    def taps_of(n, starts):
        at = pl.ds(pl.multiple_of(n * 128, 128), 128)
        weights = kernel[:, at].astype(F32)
        for start in starts:
            rows = jnp.zeros((64, 128), F32)
            for j in range(KERNEL):
                rows = rows + deep[n, pl.ds(start + j + 1, 64), :] * weights[j : j + 1, :]
            rows = residual[start : start + 64, at].astype(F32) + rows * jax.nn.sigmoid(rows)
            out[start : start + 64, at] = rows.astype(BF16)

    def inner(n, carry):
        taps_of(n, (64, 128, 192, 256))
        return carry

    def outer(n, carry):
        at = pl.ds(pl.multiple_of(n * 128, 128), 128)
        deep[n, 0:PAD, :] = jnp.where(ctx > 0, edges[0, :, at].astype(F32), 0.0)
        deep[n, PAD + ROWS :, :] = jnp.where(ctx < PARTS - 1, edges[1, :, at].astype(F32), 0.0)
        taps_of(n, (0, 320))
        return carry

    lax.fori_loop(0, D // 128, inner, 0)
    to_after.wait_recv()
    to_before.wait_recv()
    lax.fori_loop(0, D // 128, outer, 0)

    all_slots.wait_send()
    halo_copy.wait_send()
    to_after.wait_send()
    to_before.wait_send()
    for half in range(2):
        for part in range(3):

            def leave(i, carry):
                share_of(half, part, i).wait_send()
                return carry

            lax.fori_loop(1, PARTS, leave, 0)
    for gather in (gather_k, gather_v, gather_q, gather_t):
        gather.drain()


def pack_slots(mel, route, mel_wide, high, low, wide, slots):
    mel_wide[...] = mel[...].astype(F32)
    high[...] = jnp.zeros_like(high)
    low[...] = jnp.zeros_like(low)
    high[0:SLOT, :] = (route[...] // 64).astype(F32)
    low[0:SLOT, :] = (route[...] % 64).astype(F32)

    def fill(j, carry):
        to = pl.multiple_of(16 * j, 16)
        at = (SLOT * j) // 128
        wide[pl.ds(to, SLOT), :] = mel_wide[pl.ds(SLOT * j, SLOT), :]
        wide[pl.ds(to + SLOT, 2), :] = high[pl.ds(at, 2), :]
        wide[pl.ds(to + SLOT + 2, 2), :] = low[pl.ds(at, 2), :]
        return carry

    lax.fori_loop(0, RANKS, fill, 0, unroll=8)
    slots[...] = wide[...].astype(BF16).reshape(RANKS, 16, 128)


def prepare(first, second, sel, band, taps):
    row = iota((384, 512), 0)
    col = iota((384, 512), 1)
    a, m, p, r = row // 128, row % 128, col // 32, col % 32
    b = jnp.where(r >= 9, 1, 0) + jnp.where(r >= 18, 1, 0)
    hit = (r < 27) & (a == b) & (m == 8 * p - 1 + r - 9 * b)
    sel[...] = jnp.where(hit, 1.0, 0.0).astype(BF16)
    band_row = iota((128, 128), 0)
    values = first[...].astype(F32)
    for f in range(16):
        block = jnp.zeros((128, 128), F32)
        for tap in range(9):
            at = 32 * (f // 4) + 9 * (tap // 3) + 2 * (f % 4) + tap % 3
            block = jnp.where(band_row == at, values[tap : tap + 1, :], block)
        band[:, 128 * f : 128 * (f + 1)] = block.astype(BF16)
    taps[...] = jnp.zeros_like(taps)
    for position, row_tap in enumerate((1, 2, 0)):
        for o in range(2):
            for c in range(3):
                at = 640 * position + 128 * (2 * o + c)
                source = (3 * row_tap + c) * 128
                taps[at : at + 128, 128 * o : 128 * (o + 1)] = second[source : source + 128, :]


def place(me, arrived, wide, turned, sorted_rows, frames):
    wide[...] = merged(arrived[...]).astype(F32)
    for k in range(2):
        high = wide[pl.ds(SLOT + k, RANKS, stride=16), :]
        low = wide[pl.ds(SLOT + 2 + k, RANKS, stride=16), :]
        turned[128 * k : 128 * (k + 1), :] = (high * 64.0 + low).T
    position = turned[pl.ds((SLOT * me) % 128, SLOT), :]
    for r in range(SLOT):
        sorted_rows[r * RANKS : (r + 1) * RANKS, :] = wide[pl.ds(r, RANKS, stride=16), :].astype(BF16)
    target = iota((ROWS, RANKS), 0).astype(F32) * 4.0
    for k in range(4):
        chosen = jnp.concatenate(
            [
                jnp.where(position[r : r + 1, :] == target + float(k), 1.0, 0.0).astype(BF16)
                for r in range(SLOT)
            ],
            axis=1,
        )
        frames[:, 128 * k : 128 * (k + 1)] = dot(chosen, sorted_rows[...]).astype(BF16)


def block(lengths, mel, route, first, second, kernel, lin_in, wq, wk, wv, wo, pw1):
    total = ROWS + PAD
    anywhere = pl.BlockSpec(memory_space=pl.ANY)
    return pl.pallas_call(
        block_kernel,
        out_shape=[
            jax.ShapeDtypeStruct((ROWS, D), BF16),
            jax.ShapeDtypeStruct((16, 240, D), BF16),
        ],
        in_specs=[pl.BlockSpec(memory_space=pltpu.SMEM)] + [vspec()] * 5 + [anywhere] * 6,
        out_specs=[vspec(), anywhere],
        scratch_shapes=[
            VMEM((RANKS * SLOT, 128), F32),
            VMEM((16, 128), F32),
            VMEM((16, 128), F32),
            VMEM((RANKS, 16, 128), BF16),
            VMEM((RANKS, 16, 128), BF16),
            VMEM((16 * RANKS, 128), F32),
            VMEM((256, 128), F32),
            VMEM((SLOT * RANKS, 128), BF16),
            VMEM((ROWS, 512), BF16),
            VMEM((PAD, 512), BF16),
            VMEM((total, 128), F32),
            VMEM((384, 512), BF16),
            VMEM((ROWS, 512), BF16),
            VMEM((total, 512), BF16),
            VMEM((128, 2048), BF16),
            VMEM((1920, 256), BF16),
            VMEM((2, ROWS, 640), BF16),
            VMEM((2, total, 640), BF16),
            VMEM((total, 256), F32),
            VMEM((ROWS, 4096), BF16),
            VMEM((16, 256, D), BF16),
            VMEM((ROWS, D), BF16),
            VMEM((ROWS, D), BF16),
            VMEM((16, 96, 768), BF16),
            VMEM((16, 96, 768), BF16),
            VMEM((16, 96, 768), BF16),
            VMEM((3, HEADS, ROWS, 128), BF16),
            VMEM((3, HEADS, ROWS, 128), BF16),
            VMEM((HEADS, ROWS, 128), BF16),
            VMEM((HEADS, ROWS, 128), BF16),
            VMEM((240, D), BF16),
            VMEM((ROWS, D), BF16),
            VMEM((ROWS, D), BF16),
            VMEM((2, PAD, D), BF16),
            VMEM((D // 128, ROWS + 2 * PAD, 128), F32),
            DMA, DMA, DMA((16,)), DMA, DMA,
            DMA((2, 3, PARTS)), DMA((2, 3, PARTS)), DMA((PARTS,)), DMA((PARTS,)), DMA((2,)), DMA((2,)),
            DMA((4, GATHER_SENDS)), DMA((4, GATHER_RECVS)),
        ],
        compiler_params=pltpu.CompilerParams(
            vmem_limit_bytes=62 * MIB, collective_id=0, has_side_effects=True
        ),
        cost_estimate=pl.CostEstimate(
            flops=27_000_000_000, bytes_accessed=60_000_000, transcendentals=12_000_000
        ),
        name="conformer_block",
    )(lengths, mel, route, first, second, kernel, lin_in, wq, wk, wv, wo, pw1)


def local(mel_in, route, lengths, conv_first, conv_second, lin_in, wq, wk, wv, wo, pw1, dw_kernel):
    encoded, _ = block(
        lengths, mel_in, route.reshape(SLOT, 128), conv_first, conv_second, dw_kernel,
        lin_in.reshape(16, 256, D), wq, wk, wv, wo, pw1,
    )
    return encoded[None]


def solution(mesh):
    return jax.shard_map(
        local,
        mesh=mesh,
        in_specs=(
            P(("ctx", "sess"), None),
            P(("ctx", "sess")),
            P(),
            P(),
            P(),
            P(),
            P("sess", None),
            P("sess", None),
            P("sess", None),
            P("sess", None),
            P("sess", None),
            P(),
        ),
        out_specs=P("sess", "ctx", None),
        check_vma=False,
    )
```

```python
import functools
import math

import jax
import jax.numpy as jnp
from jax import lax
from jax.experimental import pallas as pl
from jax.experimental.pallas import tpu as pltpu
from jax.sharding import PartitionSpec as P

HEADS = 8
HEAD = 96
KERNEL = 31
EPS = 1e-05
ROWS = 384
PAD = 16
SLOT = 12
RANKS = 128
D = 1536
F32 = jnp.float32
BF16 = jnp.bfloat16
VMEM = pltpu.VMEM
DMA = pltpu.SemaphoreType.DMA
MESH = pl.DeviceIdType.MESH
PARTS = 8
HALF = ROWS // 2
QUARTER = HALF // 4
MIB = 1024 * 1024


def vspec():
    return pl.BlockSpec(memory_space=pltpu.VMEM)


def dot(a, b):
    return jnp.dot(a, b, preferred_element_type=F32)


def iota(shape, dim):
    return lax.broadcasted_iota(jnp.int32, shape, dim)


def layer_norm(values):
    row_mean = jnp.mean(values, axis=-1, keepdims=True)
    centred = values - row_mean
    variance = jnp.mean(centred * centred, axis=-1, keepdims=True)
    return (centred * lax.rsqrt(variance + EPS)).astype(BF16)


def remote(source, target, send, recv, device):
    return pltpu.make_async_remote_copy(
        src_ref=source, dst_ref=target, send_sem=send, recv_sem=recv, device_id=device, device_id_type=MESH
    )


class Gather:
    def __init__(self, full, base, rows, split, send, recv, here):
        ctx, sess = here
        y, z_hi = ctx // 2, ctx % 2
        z_lo, x, core = sess // 8, (sess // 2) % 4, sess % 2
        z, odd = 2 * z_hi + z_lo, y % 2

        def device(x_at, y_at, z_at, core_at):
            return (2 * y_at + z_at // 2, (z_at % 2) * 8 + x_at * 2 + core_at)

        self.next, self.prev = device((x + 1) % 4, y, z, core), device((x + 3) % 4, y, z, core)
        self.above, self.below = device(x, y, (z + 1) % 4, core), device(x, y, (z + 3) % 4, core)
        self.front, self.back = device(x, (y + 1) % 4, z, core), device(x, (y + 3) % 4, z, core)
        self.twin = device(x, y, z, 1 - core)
        near = [x, (x + 3) % 4, (x + 1) % 4, (x + 2) % 4]
        mine = [near[0] * (1 - odd) + near[2] * odd, near[1] * (1 - odd) + near[3] * odd]
        theirs = [near[0] * odd + near[2] * (1 - odd), near[1] * odd + near[3] * (1 - odd)]
        at = lambda z_at, x_at, core_at: z_at * 8 + x_at * 2 + core_at
        self.own = sess
        self.a, self.b, self.c = (at(z_lo, i, core) for i in near[1:])
        self.give = [at(z_lo, i, core) for i in mine]
        self.take = [at(1 - z_lo, i, core) for i in mine]
        self.from_y = [at(1 - z_lo, i, core) for i in theirs]
        self.from_twin = (
            [at(z_lo, i, 1 - core) for i in near]
            + [at(1 - z_lo, i, 1 - core) for i in mine]
            + [at(1 - z_lo, i, 1 - core) for i in theirs]
        )
        self.other = [at(1 - z_lo, i, core) for i in near]
        self.twin_order = [at(z, i, 1 - core) for z in (z_lo, 1 - z_lo) for i in near]
        self.full = full
        self.all = pl.ds(base, rows)
        self.low, self.high = pl.ds(base, split), pl.ds(base + split, rows - split)
        self.send_sem, self.recv_sem = send, recv
        self.sent = []

    def copy(self, shard, rows, number, recv, device):
        part = self.full.at[shard, rows]
        return remote(part, part, self.send_sem.at[number], self.recv_sem.at[recv], device)

    def send(self, shard, rows, recv, device):
        what = (shard, rows, len(self.sent), recv, device)
        self.copy(*what).start()
        self.sent.append(what)

    def wait(self, shard, rows, recv):
        self.copy(shard, rows, 0, recv, self.twin).wait_recv()

    def start(self):
        self.send(self.own, self.all, 0, self.next)
        self.send(self.own, self.all, 1, self.prev)
        self.send(self.own, self.all, 12, self.twin)

    def along_x(self):
        self.wait(self.a, self.all, 0)
        self.send(self.a, self.low, 2, self.next)
        self.wait(self.b, self.all, 1)
        self.send(self.b, self.high, 3, self.prev)
        self.send(self.give[0], self.low, 4, self.above)
        self.send(self.give[0], self.high, 5, self.below)
        self.send(self.a, self.all, 13, self.twin)
        self.send(self.b, self.all, 14, self.twin)

    def across(self):
        self.wait(self.c, self.low, 2)
        self.wait(self.c, self.high, 3)
        self.send(self.give[1], self.low, 6, self.above)
        self.send(self.give[1], self.high, 7, self.below)
        self.send(self.c, self.all, 15, self.twin)

    def along_z(self, k):
        self.wait(self.take[k], self.low, 4 + 2 * k)
        self.send(self.take[k], self.low, 16 + 2 * k, self.front)
        self.wait(self.take[k], self.high, 5 + 2 * k)
        self.send(self.take[k], self.high, 17 + 2 * k, self.back)
        self.send(self.take[k], self.all, 8 + k, self.twin)

    def along_y(self):
        for k in range(2):
            self.wait(self.from_y[k], self.low, 16 + 2 * k)
            self.wait(self.from_y[k], self.high, 17 + 2 * k)
            self.send(self.from_y[k], self.all, 10 + k, self.twin)

    def finish(self):
        for shard, recv in zip(self.from_twin, (12, 13, 14, 15, 8, 9, 10, 11)):
            self.wait(shard, self.all, recv)

    def drain(self):
        for what in self.sent:
            self.copy(*what).wait_send()


class GatherAlongX(Gather):
    def begin(self):
        self.send(self.own, self.low, 0, self.above)
        self.send(self.own, self.high, 1, self.below)
        self.send(self.own, self.all, 10, self.twin)

    def start(self):
        self.send(self.own, self.all, 2, self.next)
        self.send(self.own, self.all, 3, self.prev)

    def start_other(self):
        z = self.other
        self.wait(z[0], self.low, 0)
        self.wait(z[0], self.high, 1)
        self.send(z[0], self.all, 4, self.next)
        self.send(z[0], self.all, 5, self.prev)
        self.send(z[0], self.all, 11, self.twin)

    def along_x(self, k):
        a, b = (self.a, self.b) if k == 0 else self.other[1:3]
        self.wait(a, self.all, 2 + 2 * k)
        self.send(a, self.low, 6 + 2 * k, self.next)
        self.wait(b, self.all, 3 + 2 * k)
        self.send(b, self.high, 7 + 2 * k, self.prev)
        self.send(a, self.all, 12 + 2 * k, self.twin)
        self.send(b, self.all, 13 + 2 * k, self.twin)

    def across(self, k):
        c = self.c if k == 0 else self.other[3]
        self.wait(c, self.low, 6 + 2 * k)
        self.wait(c, self.high, 7 + 2 * k)
        self.send(c, self.all, 16 + k, self.twin)

    def finish(self):
        for shard, recv in zip(self.twin_order, (10, 12, 13, 16, 11, 14, 15, 17)):
            self.wait(shard, self.all, recv)


GATHER_SENDS = 21
GATHER_RECVS = 20


def merged(block):
    return block.reshape(block.shape[0] * block.shape[1], block.shape[2])


def block_kernel(
    lengths, mel, route, first, second, kernel, lin_hbm, wq, wk, wv, wo, pw1,
    out, tail_full,
    mel_wide, high, low, slots, arrived, wide, turned, sorted_rows, frames, halo, last, sel, win_e, win_o,
    band, taps, even, odd, behind, sub, big, emb, normed, w_q, w_k, w_v, packed, shares, packed_q, shares_q, held, context, heads, tail_own,
    residual, gated, edges, deep,
    mel_send, mel_recv, local_sem, halo_send, halo_recv,
    share_send, share_recv, query_send, query_recv, head_send, head_recv, edge_send, edge_recv, gather_send, gather_recv,
):
    ctx, sess = lax.axis_index("ctx"), lax.axis_index("sess")
    me = ctx * 16 + sess
    total = ROWS + PAD
    here = (ctx, sess)
    after, before = ((ctx + 1) % PARTS, sess), ((ctx + PARTS - 1) % PARTS, sess)
    live_rows = lengths[sess] - ctx * ROWS

    barrier = pltpu.get_barrier_semaphore()

    def greet(i, carry):
        other = lax.rem(me + i, RANKS)
        pl.semaphore_signal(barrier, inc=1, device_id=(other // 16, other % 16), device_id_type=MESH)
        return carry

    lax.fori_loop(1, RANKS, greet, 0)
    own_copies = [
        pltpu.make_async_copy(source, target, local_sem.at[i])
        for i, (source, target) in enumerate(
            [
                (wk, w_k.at[sess]),
                (wv, w_v.at[sess]),
                (wq, w_q.at[sess]),
                (pw1.at[:, 0:D], tail_own.at[0:96]),
                (pw1.at[:, D : 2 * D], tail_own.at[96:192]),
                (wo, tail_own.at[192:240]),
                (lin_hbm, big),
            ]
        )
    ]
    for copy in own_copies:
        copy.start()
    lin_copy = own_copies[6]
    pack_slots(mel, route, mel_wide, high, low, wide, slots)
    own_slot = pltpu.make_async_copy(slots.at[me], arrived.at[me], local_sem.at[7])
    own_slot.start()
    prepare(first, second, sel, band, taps)
    gather_k, gather_v, gather_q, gather_t = (
        kind(full, base, rows, split, gather_send.at[i], gather_recv.at[i], here)
        for i, (kind, full, base, rows, split) in enumerate(
            [
                (Gather, w_k, 0, 96, 48),
                (Gather, w_v, 0, 96, 48),
                (Gather, w_q, 0, 96, 48),
                (GatherAlongX, tail_full, 0, 240, 128),
            ]
        )
    )
    for copy in own_copies[:6]:
        copy.wait()
    own_tail = pltpu.make_async_copy(tail_own, tail_full.at[sess], local_sem.at[3])
    own_tail.start()
    pl.semaphore_wait(barrier, RANKS - 1)

    def deliver(i, carry):
        other = lax.rem(me + i, RANKS)
        remote(slots.at[other], arrived.at[me], mel_send, mel_recv, (other // 16, other % 16)).start()
        return carry

    lax.fori_loop(1, RANKS, deliver, 0)
    gather_k.start()
    gather_v.start()
    gather_q.start()
    own_slot.wait()
    own_tail.wait()
    gather_t.begin()
    all_slots = remote(slots.at[0 : RANKS - 1], arrived.at[0 : RANKS - 1], mel_send, mel_recv, after)
    all_slots.wait_recv()

    place(me, arrived, wide, turned, sorted_rows, frames)
    halo_copy = remote(frames.at[ROWS - PAD :], halo, halo_send, halo_recv, after)
    halo_copy.start()
    gather_k.along_x()
    win_o[PAD:total, :] = dot(frames[:, 128:512], sel[...]).astype(BF16)
    halo_copy.wait_recv()
    first_rows = jnp.where(ctx > 0, halo[...].astype(F32), 0.0)
    last[0:PAD, :] = first_rows[:, 384:512]
    last[PAD:total, :] = frames[:, 384:512].astype(F32)
    previous = last[pl.ds(PAD - 1, ROWS), :].astype(BF16)
    win_e[...] = dot(jnp.concatenate([previous, frames[:, 0:256]], axis=1), sel[...]).astype(BF16)
    win_o[0:PAD, :] = dot(first_rows.astype(BF16)[:, 128:512], sel[...]).astype(BF16)
    gather_v.along_x()

    plan = [
        [gather_k.across, lambda: gather_k.along_z(0), gather_q.along_x],
        [gather_v.across, lambda: gather_v.along_z(0), gather_t.start],
        [gather_q.across, lambda: gather_q.along_z(0), lambda: gather_k.along_z(1)],
        [lambda: gather_v.along_z(1), gather_t.start_other],
        [lambda: gather_q.along_z(1), gather_k.along_y],
        [gather_v.along_y],
        [],
        [gather_q.along_y],
    ]

    def four_bins(g, side):
        q = pl.ds(pl.multiple_of((g // 4) * 128, 128), 128)
        weights = band[:, pl.ds(pl.multiple_of((g % 4) * 512, 512), 512)]
        even[side, :, 128:640] = jnp.maximum(dot(win_e[:, q], weights), 0.0).astype(BF16)
        odd[side, :, 128:640] = jnp.maximum(dot(win_o[:, q], weights), 0.0).astype(BF16)
        even[1 - side, :, 0:128] = even[side, :, 512:640]
        odd[1 - side, :, 0:128] = odd[side, :, 512:640]

    def two_bins(g, side):
        behind[...] = dot(odd[side], taps[1280:1920, :])
        both = jnp.concatenate([even[side], odd[side, PAD:, :]], axis=1)
        rows = dot(both, taps[0:1280, :]) + behind[pl.ds(PAD - 1, ROWS), :]
        sub[:, pl.ds(pl.multiple_of(g * 256, 256), 256)] = jnp.maximum(rows, 0.0).astype(BF16)

    def groups(i, carry):
        four_bins(2 * i, 0)
        two_bins(2 * i, 0)
        four_bins(2 * i + 1, 1)
        two_bins(2 * i + 1, 1)
        for step, actions in enumerate(plan):

            @pl.when(i == step)
            def _():
                for action in actions:
                    action()

        return carry

    even[0, :, 0:128] = jnp.zeros((ROWS, 128), BF16)
    odd[0, :, 0:128] = jnp.zeros((total, 128), BF16)
    lax.fori_loop(0, 8, groups, 0)
    lin_copy.wait()

    def rows_of(half, carry):
        start = pl.multiple_of(half * HALF, HALF)
        mine = pl.ds(start, HALF)

        def project(n, carry):
            at = pl.ds(pl.multiple_of(n * 512, 512), 512)
            emb[mine, at] = dot(sub[mine, :], merged(big[:, :, at])).astype(BF16)
            return carry

        lax.fori_loop(0, 3, project, 0)
        normed[mine, :] = layer_norm(emb[mine, :].astype(F32))

        @pl.when(half == 0)
        def _():
            gather_k.finish()
            gather_v.finish()

        for part, weights in ((0, w_k), (1, w_v)):
            rows = dot(normed[mine, :], merged(weights[...]))
            for h in range(HEADS):
                packed[part, half, h] = packed_head(rows, h)

            def share(i, carry):
                share_of(half, part, i).start()
                return carry

            lax.fori_loop(1, PARTS, share, 0)
        return carry

    def share_of(half, part, i):
        other = lax.rem(ctx + i, PARTS)
        return remote(
            packed.at[part, half, other], shares.at[part, half, ctx],
            share_send.at[half, part, i], share_recv.at[half, part, i], (other, sess),
        )

    def queries_for(i):
        other = lax.rem(ctx + i, PARTS)
        return remote(
            packed_q.at[other], shares_q.at[ctx], query_send.at[i], query_recv.at[i], (other, sess)
        )

    lax.fori_loop(0, 2, rows_of, 0)
    gather_q.finish()
    for half in range(2):
        rows = dot(normed[half * HALF : (half + 1) * HALF, :], merged(w_q[...]))
        for h in range(HEADS):
            packed_q[h, half] = packed_head(rows, h)
    own_queries = pltpu.make_async_copy(packed_q.at[ctx], shares_q.at[ctx], local_sem.at[8])
    own_queries.start()

    def ask(i, carry):
        queries_for(i).start()
        return carry

    lax.fori_loop(1, PARTS, ask, 0)
    gather_t.along_x(0)

    def land(half, part, block, source):
        def extra(row):
            if part == 1:
                return jnp.ones((QUARTER, 128), F32)
            first_row = source * ROWS + half * HALF + row
            live = iota((QUARTER, 128), 0) < lengths[sess] - first_row
            return jnp.where(live, 0.0, -1e30)

        for q, rows in enumerate(unpacked_head(block, extra)):
            held[part, source, half * HALF + q * QUARTER : half * HALF + (q + 1) * QUARTER, :] = rows

    for half in range(2):
        for part in range(2):
            land(half, part, packed[part, half, ctx], ctx)
    own_queries.wait()
    for half in range(2):
        for part in range(2):

            def arrive(i, carry):
                share_of(half, part, i).wait_recv()
                source = lax.rem(ctx + PARTS - i, PARTS)
                land(half, part, shares[part, half, source], source)
                return carry

            lax.fori_loop(1, PARTS, arrive, 0)

    scale = math.log2(math.e) / math.sqrt(HEAD)

    def attend(i):
        other = lax.rem(ctx + PARTS - i, PARTS)
        keys, values = merged(held[0]), merged(held[1])
        ones = lambda row: jnp.ones((QUARTER, 128), F32)
        for half in range(2):
            at = pl.ds(half * HALF, HALF)
            queries = jnp.concatenate(unpacked_head(shares_q[other, half], ones), axis=0)
            scores = lax.dot_general(
                queries, keys, (((1,), (1,)), ((), ())), preferred_element_type=F32
            )
            row_max = jnp.max(scores, axis=1, keepdims=True)
            weights = jnp.exp2((scores - row_max) * scale).astype(BF16)
            summed = dot(weights, values)
            result = summed / summed[:, HEAD : HEAD + 1]
            result = jnp.where(iota(result.shape, 1) < HEAD, result, 0.0)
            context[other, at, :] = result.astype(BF16)

    def head_of(i):
        other = lax.rem(ctx + PARTS - i, PARTS)
        return remote(
            context.at[other], heads.at[ctx], head_send.at[i], head_recv.at[i], (other, sess)
        )

    later = {
        3: [lambda: gather_t.along_x(1)],
        4: [lambda: gather_t.across(0)],
        7: [lambda: gather_t.across(1), gather_t.finish],
    }
    tail_copy = pltpu.make_async_copy(tail_full, big.at[:, 0:240, :], local_sem.at[14])
    later[7].append(tail_copy.start)

    def attend_for(i, carry):
        @pl.when(i < PARTS)
        def _():
            queries_for(i).wait_recv()

        attend(i)

        @pl.when(i < PARTS)
        def _():
            head_of(i).start()

        for at, actions in later.items():

            @pl.when(i == at)
            def _():
                for action in actions:
                    action()

        return carry

    lax.fori_loop(1, PARTS + 1, attend_for, 0)
    own_head = pltpu.make_async_copy(context.at[ctx], heads.at[ctx], local_sem.at[15])
    own_head.start()
    own_head.wait()

    def arrive_heads(i, carry):
        head_of(i).wait()
        return carry

    lax.fori_loop(1, PARTS, arrive_heads, 0)
    tail_copy.wait()

    w_out = merged(big[:, 192:240, :])
    summed = emb[...].astype(F32)
    for pair in range(4):
        left = jnp.concatenate([heads[2 * pair], heads[2 * pair + 1]], axis=1)
        at = 192 * pair
        pad = jnp.zeros((32, D), BF16)
        right = jnp.concatenate([w_out[at : at + 96], pad, w_out[at + 96 : at + 192], pad], axis=0)
        summed = summed + dot(left, right)
    residual[...] = summed.astype(BF16)
    normed[...] = layer_norm(residual[...].astype(F32))
    live = iota((ROWS, 256), 0) < live_rows

    def lift(n, carry):
        at = pl.ds(pl.multiple_of(n * 256, 256), 256)
        value = dot(normed[...], merged(big[:, 0:96, at]))
        gate = dot(normed[...], merged(big[:, 96:192, at]))
        rows = jnp.where(live, value * jax.nn.sigmoid(gate), 0.0).astype(BF16)
        gated[:, at] = rows
        wide_rows = rows.astype(F32)
        deep[2 * n, PAD : PAD + ROWS, :] = wide_rows[:, 0:128]
        deep[2 * n + 1, PAD : PAD + ROWS, :] = wide_rows[:, 128:256]
        return carry

    lax.fori_loop(0, 6, lift, 0)
    to_after = remote(gated.at[ROWS - PAD :], edges.at[0], edge_send.at[0], edge_recv.at[0], after)
    to_before = remote(gated.at[0:PAD], edges.at[1], edge_send.at[1], edge_recv.at[1], before)
    to_after.start()
    to_before.start()

    def taps_of(n, starts):
        at = pl.ds(pl.multiple_of(n * 128, 128), 128)
        weights = kernel[:, at].astype(F32)
        for start in starts:
            rows = jnp.zeros((64, 128), F32)
            for j in range(KERNEL):
                rows = rows + deep[n, pl.ds(start + j + 1, 64), :] * weights[j : j + 1, :]
            rows = residual[start : start + 64, at].astype(F32) + rows * jax.nn.sigmoid(rows)
            out[start : start + 64, at] = rows.astype(BF16)

    def inner(n, carry):
        taps_of(n, (64, 128, 192, 256))
        return carry

    def outer(n, carry):
        at = pl.ds(pl.multiple_of(n * 128, 128), 128)
        deep[n, 0:PAD, :] = jnp.where(ctx > 0, edges[0, :, at].astype(F32), 0.0)
        deep[n, PAD + ROWS :, :] = jnp.where(ctx < PARTS - 1, edges[1, :, at].astype(F32), 0.0)
        taps_of(n, (0, 320))
        return carry

    lax.fori_loop(0, D // 128, inner, 0)
    to_after.wait_recv()
    to_before.wait_recv()
    lax.fori_loop(0, D // 128, outer, 0)

    all_slots.wait_send()
    halo_copy.wait_send()
    to_after.wait_send()
    to_before.wait_send()
    for half in range(2):
        for part in range(2):

            def leave(i, carry):
                share_of(half, part, i).wait_send()
                return carry

            lax.fori_loop(1, PARTS, leave, 0)

    def asked(i, carry):
        queries_for(i).wait_send()
        return carry

    lax.fori_loop(1, PARTS, asked, 0)
    for gather in (gather_k, gather_v, gather_q, gather_t):
        gather.drain()


def packed_head(rows, h):
    base, shift = (HEAD * h) // 128 * 128, (HEAD * h) % 128
    if shift == 0:
        head = rows[:, base : base + 128]
    elif shift == 32:
        head = pltpu.roll(rows[:, base : base + 128], 128 - shift, 1)
    else:
        head = pltpu.roll(rows[:, base : base + 256], 256 - shift, 1)[:, 0:128]
    lane = iota((QUARTER, 128), 1)
    last = head[3 * QUARTER :]
    quarters = [
        jnp.where(lane < HEAD, head[q * QUARTER : (q + 1) * QUARTER], pltpu.roll(last, HEAD - 32 * q, 1))
        for q in range(3)
    ]
    return jnp.concatenate(quarters, axis=0).astype(BF16)


def unpacked_head(block, extra):
    block = block.astype(F32)
    quarters = [block[q * QUARTER : (q + 1) * QUARTER] for q in range(3)]
    lane = iota((QUARTER, 128), 1)
    pieces = [pltpu.roll(quarters[q], 32 * q + 32, 1) for q in range(3)]
    quarters.append(jnp.where(lane < 32, pieces[0], jnp.where(lane < 64, pieces[1], pieces[2])))
    return [
        jnp.where(lane < HEAD, rows, jnp.where(lane == HEAD, extra(q * QUARTER), 0.0)).astype(BF16)
        for q, rows in enumerate(quarters)
    ]


def pack_slots(mel, route, mel_wide, high, low, wide, slots):
    mel_wide[...] = mel[...].astype(F32)
    high[...] = jnp.zeros_like(high)
    low[...] = jnp.zeros_like(low)
    high[0:SLOT, :] = (route[...] // 64).astype(F32)
    low[0:SLOT, :] = (route[...] % 64).astype(F32)

    def fill(j, carry):
        to = pl.multiple_of(16 * j, 16)
        at = (SLOT * j) // 128
        wide[pl.ds(to, SLOT), :] = mel_wide[pl.ds(SLOT * j, SLOT), :]
        wide[pl.ds(to + SLOT, 2), :] = high[pl.ds(at, 2), :]
        wide[pl.ds(to + SLOT + 2, 2), :] = low[pl.ds(at, 2), :]
        return carry

    lax.fori_loop(0, RANKS, fill, 0, unroll=8)
    slots[...] = wide[...].astype(BF16).reshape(RANKS, 16, 128)


def prepare(first, second, sel, band, taps):
    row = iota((384, 512), 0)
    col = iota((384, 512), 1)
    a, m, p, r = row // 128, row % 128, col // 32, col % 32
    b = jnp.where(r >= 9, 1, 0) + jnp.where(r >= 18, 1, 0)
    hit = (r < 27) & (a == b) & (m == 8 * p - 1 + r - 9 * b)
    sel[...] = jnp.where(hit, 1.0, 0.0).astype(BF16)
    band_row = iota((128, 128), 0)
    values = first[...].astype(F32)
    for f in range(16):
        block = jnp.zeros((128, 128), F32)
        for tap in range(9):
            at = 32 * (f // 4) + 9 * (tap // 3) + 2 * (f % 4) + tap % 3
            block = jnp.where(band_row == at, values[tap : tap + 1, :], block)
        band[:, 128 * f : 128 * (f + 1)] = block.astype(BF16)
    taps[...] = jnp.zeros_like(taps)
    for position, row_tap in enumerate((1, 2, 0)):
        for o in range(2):
            for c in range(3):
                at = 640 * position + 128 * (2 * o + c)
                source = (3 * row_tap + c) * 128
                taps[at : at + 128, 128 * o : 128 * (o + 1)] = second[source : source + 128, :]


def place(me, arrived, wide, turned, sorted_rows, frames):
    wide[...] = merged(arrived[...]).astype(F32)
    for k in range(2):
        high = wide[pl.ds(SLOT + k, RANKS, stride=16), :]
        low = wide[pl.ds(SLOT + 2 + k, RANKS, stride=16), :]
        turned[128 * k : 128 * (k + 1), :] = (high * 64.0 + low).T
    position = turned[pl.ds((SLOT * me) % 128, SLOT), :]
    for r in range(SLOT):
        sorted_rows[r * RANKS : (r + 1) * RANKS, :] = wide[pl.ds(r, RANKS, stride=16), :].astype(BF16)
    target = iota((ROWS, RANKS), 0).astype(F32) * 4.0
    for k in range(4):
        chosen = jnp.concatenate(
            [
                jnp.where(position[r : r + 1, :] == target + float(k), 1.0, 0.0).astype(BF16)
                for r in range(SLOT)
            ],
            axis=1,
        )
        frames[:, 128 * k : 128 * (k + 1)] = dot(chosen, sorted_rows[...]).astype(BF16)


def block(lengths, mel, route, first, second, kernel, lin_in, wq, wk, wv, wo, pw1):
    total = ROWS + PAD
    anywhere = pl.BlockSpec(memory_space=pl.ANY)
    return pl.pallas_call(
        block_kernel,
        out_shape=[
            jax.ShapeDtypeStruct((ROWS, D), BF16),
            jax.ShapeDtypeStruct((16, 240, D), BF16),
        ],
        in_specs=[pl.BlockSpec(memory_space=pltpu.SMEM)] + [vspec()] * 5 + [anywhere] * 6,
        out_specs=[vspec(), anywhere],
        scratch_shapes=[
            VMEM((RANKS * SLOT, 128), F32),
            VMEM((16, 128), F32),
            VMEM((16, 128), F32),
            VMEM((RANKS, 16, 128), BF16),
            VMEM((RANKS, 16, 128), BF16),
            VMEM((16 * RANKS, 128), F32),
            VMEM((256, 128), F32),
            VMEM((SLOT * RANKS, 128), BF16),
            VMEM((ROWS, 512), BF16),
            VMEM((PAD, 512), BF16),
            VMEM((total, 128), F32),
            VMEM((384, 512), BF16),
            VMEM((ROWS, 512), BF16),
            VMEM((total, 512), BF16),
            VMEM((128, 2048), BF16),
            VMEM((1920, 256), BF16),
            VMEM((2, ROWS, 640), BF16),
            VMEM((2, total, 640), BF16),
            VMEM((total, 256), F32),
            VMEM((ROWS, 4096), BF16),
            VMEM((16, 256, D), BF16),
            VMEM((ROWS, D), BF16),
            VMEM((ROWS, D), BF16),
            VMEM((16, 96, 768), BF16),
            VMEM((16, 96, 768), BF16),
            VMEM((16, 96, 768), BF16),
            VMEM((2, 2, HEADS, 3 * QUARTER, 128), BF16),
            VMEM((2, 2, PARTS, 3 * QUARTER, 128), BF16),
            VMEM((HEADS, 2, 3 * QUARTER, 128), BF16),
            VMEM((PARTS, 2, 3 * QUARTER, 128), BF16),
            VMEM((2, PARTS, ROWS, 128), BF16),
            VMEM((HEADS, ROWS, 128), BF16),
            VMEM((HEADS, ROWS, 128), BF16),
            VMEM((240, D), BF16),
            VMEM((ROWS, D), BF16),
            VMEM((ROWS, D), BF16),
            VMEM((2, PAD, D), BF16),
            VMEM((D // 128, ROWS + 2 * PAD, 128), F32),
            DMA, DMA, DMA((16,)), DMA, DMA,
            DMA((2, 2, PARTS)), DMA((2, 2, PARTS)), DMA((PARTS,)), DMA((PARTS,)),
            DMA((PARTS,)), DMA((PARTS,)), DMA((2,)), DMA((2,)),
            DMA((4, GATHER_SENDS)), DMA((4, GATHER_RECVS)),
        ],
        compiler_params=pltpu.CompilerParams(
            vmem_limit_bytes=62 * MIB, collective_id=0, has_side_effects=True
        ),
        cost_estimate=pl.CostEstimate(
            flops=27_000_000_000, bytes_accessed=60_000_000, transcendentals=12_000_000
        ),
        name="conformer_block",
    )(lengths, mel, route, first, second, kernel, lin_in, wq, wk, wv, wo, pw1)


def local(mel_in, route, lengths, conv_first, conv_second, lin_in, wq, wk, wv, wo, pw1, dw_kernel):
    encoded, _ = block(
        lengths, mel_in, route.reshape(SLOT, 128), conv_first, conv_second, dw_kernel,
        lin_in.reshape(16, 256, D), wq, wk, wv, wo, pw1,
    )
    return encoded[None]


def solution(mesh):
    return jax.shard_map(
        local,
        mesh=mesh,
        in_specs=(
            P(("ctx", "sess"), None),
            P(("ctx", "sess")),
            P(),
            P(),
            P(),
            P(),
            P("sess", None),
            P("sess", None),
            P("sess", None),
            P("sess", None),
            P("sess", None),
            P(),
        ),
        out_specs=P("sess", "ctx", None),
        check_vma=False,
    )
```
